128 devices in a mesh: gx: 4 (over z), gy: 4 (over x), gz: 8 (over y, core).
Axes of the slice: x: 4, y: 4, z: 4, core: 2. Of those that a mesh axis runs over, the one named last changes fastest.
Arguments:
- volume: float32 [1024, 512, 1024], P('gx', 'gz', 'gy'), may hold values from -40 to 40
- sketch_a: float32 [1024, 256], P('gy'), may hold values from -0.1875 to 0.1875
- sketch_b: float32 [512, 256], P('gz'), may hold values from -0.25 to 0.25
- sketch_c: float32 [256, 256], replicated, may hold values from -0.375 to 0.375
- sketch_d: float32 [512, 256], P('gz'), may hold values from -0.25 to 0.25
Outputs:
- q_first: float32 [1024, 256], P('gx')
- q_second: float32 [1024, 256], P('gy')
- core: float32 [256, 512, 256], P(('gx', 'gy'), 'gz')
The draws below stay inside these ranges and needn't reach their ends.
All inputs are finite; a program needn't handle non-finite values.
Results may differ from the reference program's by a relative error of at most 0.00019.
Values sent between devices are 32-bit elements; how exact they have to be, the bound alone decides.
No kernel may reach another device: no remote copies, remote signals or barrier semaphores. Data moves between devices by JAX's collectives and lax.ppermute only.
A program may use at most 128 MiB of HBM per device.

```python
import math
import jax
import jax.numpy as jnp
from jax import lax

CX = 256
R1 = 256
R2 = 256
N1 = 1024
N2 = 1024
N3 = 512
N_GX = 4


def draw_volume(key, part):
    key = jax.random.fold_in(key, 7)
    keys = jax.random.split(key, 4)
    ramp = 1.0 + 2.0 * jnp.arange(N1, dtype=jnp.float32) / (N1 - 1)
    base = jax.random.truncated_normal(keys[0], -4.0, 4.0, (N1, N3, N2), jnp.float32)
    spread_log = math.log(3.0)
    divisor = 12.0
    row_scale = ramp * jnp.exp(spread_log * jax.random.uniform(keys[1], (N1,), jnp.float32))
    depth_scale = jnp.exp(spread_log * jax.random.uniform(keys[2], (N3,), jnp.float32))
    column_scale = jnp.exp(spread_log * jax.random.uniform(keys[3], (N2,), jnp.float32))
    scaled = base * row_scale[:, None, None] * depth_scale[None, :, None] * column_scale[None, None, :]
    return scaled / divisor


def levels(rng, shape, cuts, low, top_value):
    def one(axis_at, blocks):
        steps = jax.random.uniform(jax.random.fold_in(jax.random.fold_in(rng, 6), axis_at), (blocks,), jnp.float32, low / len(cuts), top_value / len(cuts))
        return jnp.repeat(jnp.exp(steps), shape[axis_at] // blocks).reshape((-1,) + (1,) * (len(shape) - axis_at - 1))

    level = one(*cuts[0])
    for cut in cuts[1:]:
        level = level * one(*cut)
    return level


def noise(key, dims, scale, limit, shards=(), kind=jnp.bfloat16):
    array = scale * jax.random.normal(key, dims, jnp.float32)
    if shards:
        array = array * levels(key, dims, shards, -0.22, 0.18)
    return jnp.clip(array, -limit, limit).astype(kind)


def setup_inputs(seed: int = 0) -> dict:
    arg_keys = jax.random.split(jax.random.key(seed), 6)
    volume = draw_volume(jax.random.fold_in(arg_keys[5], 71), 0)
    sketch_a = noise(arg_keys[1], (N2, R1), N2 ** -0.5, 0.1875, ((0, 4),), jnp.float32)
    sketch_b = noise(arg_keys[2], (N3, R1), N3 ** -0.5, 0.25, ((0, 8),), jnp.float32)
    sketch_c = noise(arg_keys[3], (R1, R2), R1 ** -0.5, 0.375, (), jnp.float32)
    sketch_d = noise(arg_keys[4], (N3, R2), N3 ** -0.5, 0.25, ((0, 8),), jnp.float32)
    return {"volume": volume, "sketch_a": sketch_a, "sketch_b": sketch_b, "sketch_c": sketch_c, "sketch_d": sketch_d}


def orthonormal(rows):
    gram = jnp.dot(rows.T.astype(jnp.float32), rows.astype(jnp.float32), precision=lax.Precision.HIGHEST, preferred_element_type=jnp.float32)
    lower = jnp.linalg.cholesky(gram)
    return lax.linalg.triangular_solve(lower, rows, left_side=False, lower=True, transpose_a=True)

def reference(volume, sketch_a, sketch_b, sketch_c, sketch_d):
    highest = lax.Precision.HIGHEST
    blocks = volume.reshape(N_GX, CX, N3, N2)

    def sketch_block(block):
        spread = jnp.dot(block.reshape(CX * N3, N2).astype(jnp.float32), sketch_a.astype(jnp.float32), precision=highest, preferred_element_type=jnp.float32)
        return jnp.einsum('ikp,kp->ip', spread.reshape(CX, N3, R1), sketch_b, precision=highest)
    sketch_first = lax.map(sketch_block, blocks).reshape(N1, R1)
    q_first = orthonormal(sketch_first)
    truncated = jnp.dot(q_first.T.astype(jnp.float32), volume.reshape(N1, N3 * N2).astype(jnp.float32), precision=highest, preferred_element_type=jnp.float32)
    mixed = jnp.dot(sketch_c.T.astype(jnp.float32), truncated.astype(jnp.float32), precision=highest, preferred_element_type=jnp.float32)
    sketch_second = jnp.einsum('qkj,kq->jq', mixed.reshape(R2, N3, N2), sketch_d, precision=highest)
    q_second = orthonormal(sketch_second)
    core = jnp.dot(truncated.reshape(R1 * N3, N2).astype(jnp.float32), q_second.astype(jnp.float32), precision=highest, preferred_element_type=jnp.float32)
    return (q_first, q_second, core.reshape(R1, N3, R2))
```

```python
import functools

import jax
import jax.numpy as jnp
from jax import lax
from jax.experimental import pallas as pl
from jax.experimental.pallas import tpu as pltpu
from jax.sharding import PartitionSpec as P

HIGHEST = lax.Precision.HIGHEST
LANES = 128
PANEL = 32
GROUP = 16
VMEM_BYTES = 28 * 2**20
SMALL = pl.CostEstimate(flops=2**20, bytes_accessed=2**16, transcendentals=0)
SENT = [(kind, shift, shift == 2) for kind in (0, 1) for shift in (1, 2, 3)]


def dot_f32(a, b, contract):
    return lax.dot_general(
        a, b, (contract, ((), ())), precision=HIGHEST, preferred_element_type=jnp.float32
    )


def factor_inverse(work, inverse):
    n = work.shape[0]
    halves = n // LANES
    rows_at = lax.broadcasted_iota(jnp.int32, (n, n), 0)
    columns_at = lax.broadcasted_iota(jnp.int32, (n, n), 1)
    inverse[...] = jnp.where(rows_at == columns_at, 1.0, 0.0)
    row = lax.broadcasted_iota(jnp.int32, (PANEL, LANES), 0)
    for top in range(0, n, PANEL):
        half = top // LANES
        left = half * LANES
        bottom = top + PANEL
        tiles = [work[top:bottom, t * LANES : (t + 1) * LANES] for t in range(half, halves)]
        tiles += [inverse[top:bottom, t * LANES : (t + 1) * LANES] for t in range(half + 1)]
        pivots = jnp.ones((PANEL, LANES), jnp.float32)
        for start in range(0, PANEL, GROUP):
            first = top - left + start
            columns = [
                jnp.broadcast_to(tiles[0][:, first + m : first + m + 1], (PANEL, LANES))
                for m in range(GROUP)
            ]
            for m in range(GROUP):
                at = start + m
                pivot = columns[m][at : at + 1, :]
                pivots = jnp.where(row == at, pivot, pivots)
                factor = jnp.where(row > at, columns[m] * (1.0 / pivot), 0.0)
                for later in range(m + 1, GROUP):
                    columns[later] = columns[later] - factor * columns[later][at : at + 1, :]
                tiles = [tile - factor * tile[at : at + 1, :] for tile in tiles]
        scale = lax.rsqrt(pivots)
        tiles = [tile * scale for tile in tiles]
        kept = halves - half
        for t in range(half + 1):
            inverse[top:bottom, t * LANES : (t + 1) * LANES] = tiles[kept + t]
        if bottom < n:
            upper = jnp.concatenate(tiles[:kept], 1)
            solved = jnp.concatenate(tiles[kept:], 1)
            lower = upper.T[bottom - left :, :]
            work[bottom:, left:] = work[bottom:, left:] - dot_f32(lower, upper, ((1,), (0,)))
            inverse[bottom:, : left + LANES] = inverse[bottom:, : left + LANES] - dot_f32(
                lower, solved, ((1,), (0,))
            )


def split(x):
    high = x.astype(jnp.bfloat16)
    return high, (x - high.astype(jnp.float32)).astype(jnp.bfloat16)


def left_parts(x):
    high, low = split(x)
    return jnp.concatenate([high, high, low], 1)


def right_parts(x):
    high, low = split(x)
    return jnp.concatenate([high, low, high], 0)


def dot_parts(a, b):
    return jnp.dot(a, b, preferred_element_type=jnp.float32)


def place_rows(core, shares_ref, others_ref, all_ref):
    half = shares_ref.shape[1]
    for at in range(4):
        top = at * 2 * half
        mine = pl.multiple_of(top + core * half, half)
        other = pl.multiple_of(top + (1 - core) * half, half)
        all_ref[pl.ds(mine, half), :] = shares_ref[at]
        all_ref[pl.ds(other, half), :] = others_ref[at]


def first_orthonormal_kernel(place, *refs):
    shares, others, c_ref, q_ref, folded_ref, inverse_ref, all_ref, work = refs
    place_rows(place[2], shares, others, all_ref)
    rows = all_ref[...]
    n = rows.shape[1]
    work[...] = dot_f32(rows, rows, ((0,), (0,)))
    factor_inverse(work, inverse_ref)
    q = dot_f32(rows[:n], inverse_ref[...], ((1,), (1,)))
    q_ref[...] = q
    folded_ref[...] = dot_f32(c_ref[...], q, ((0,), (1,)))


def first_orthonormal(place, shares, sketch_c):
    _, half, n = shares[0].shape
    square = jax.ShapeDtypeStruct((n, n), jnp.float32)
    return pl.pallas_call(
        first_orthonormal_kernel,
        in_specs=[pl.BlockSpec(memory_space=pltpu.SMEM)]
        + [pl.BlockSpec(memory_space=pltpu.VMEM)] * 3,
        out_shape=[square] * 3 + [jax.ShapeDtypeStruct((8 * half, n), jnp.float32)],
        scratch_shapes=[pltpu.VMEM((n, n), jnp.float32)],
        compiler_params=pltpu.CompilerParams(vmem_limit_bytes=VMEM_BYTES),
        cost_estimate=SMALL,
        name="first_orthonormal",
    )(place, *shares, sketch_c)


def second_orthonormal_kernel(place, *refs):
    shares, others, q_ref, q_all_ref, all_ref, work, inverse = refs
    place_rows(place[2], shares, others, all_ref)
    rows = all_ref[...]
    n = rows.shape[1]
    work[...] = dot_f32(rows, rows, ((0,), (0,)))
    factor_inverse(work, inverse)
    q = dot_f32(rows, inverse[...], ((1,), (1,)))
    q_ref[...] = q[:n]
    q_all_ref[...] = q


def second_orthonormal(place, shares):
    _, half, n = shares[0].shape
    return pl.pallas_call(
        second_orthonormal_kernel,
        in_specs=[pl.BlockSpec(memory_space=pltpu.SMEM)]
        + [pl.BlockSpec(memory_space=pltpu.VMEM)] * 2,
        out_shape=[
            jax.ShapeDtypeStruct((n, n), jnp.float32),
            jax.ShapeDtypeStruct((8 * half, n), jnp.float32),
        ],
        scratch_shapes=[
            pltpu.VMEM((8 * half, n), jnp.float32),
            pltpu.VMEM((n, n), jnp.float32),
            pltpu.VMEM((n, n), jnp.float32),
        ],
        compiler_params=pltpu.CompilerParams(vmem_limit_bytes=VMEM_BYTES),
        cost_estimate=SMALL,
        name="second_orthonormal",
    )(place, *shares)


def first_sketch_kernel(place, v_ref, a_ref, b_ref, kept_ref, given_ref, *refs):
    sent, (parts, rows_ref, sems) = refs[: len(SENT)], refs[len(SENT) :]
    rows, depth, cols = v_ref.shape
    step = pl.program_id(0)
    steps = pl.num_programs(0)

    @pl.when(step == 0)
    def _():
        parts[...] = right_parts(a_ref[...])

    half_steps = steps // 2
    at = pl.ds(pl.multiple_of(lax.rem(step, half_steps) * rows, rows), rows)

    def copy_out(key):
        kind, shift, second = SENT[key]
        target = lax.rem(place[1 - kind] + shift, 4) * 8 + 32 * kind
        rows_at = at if second else pl.ds(pl.multiple_of(step * rows, rows), rows)
        return pltpu.make_async_copy(
            v_ref.at[:, pl.ds(pl.multiple_of(target, 8), 8), :], sent[key].at[rows_at], sems.at[key]
        )

    whole = [key for key, (_, _, second) in enumerate(SENT) if not second]
    late = [key for key, (_, _, second) in enumerate(SENT) if second]
    for key in whole:
        copy_out(key).start()

    @pl.when(step >= half_steps)
    def _():
        for key in late:
            copy_out(key).start()

    flat = v_ref.reshape(rows * depth, cols)
    weights = b_ref[...]
    for top in range(0, rows, 8):
        spread = dot_parts(left_parts(flat[top * depth : (top + 8) * depth, :]), parts[...])
        rows_ref[top : top + 8, :] = jnp.sum(spread.reshape(8, depth, -1) * weights[None], axis=1)

    @pl.when(step // half_steps == place[2])
    def _():
        kept_ref[at, :] = rows_ref[...]

    @pl.when(step // half_steps != place[2])
    def _():
        given_ref[at, :] = rows_ref[...]

    for key in whole:
        copy_out(key).wait()

    @pl.when(step >= half_steps)
    def _():
        for key in late:
            copy_out(key).wait()


def first_sketch(place, volume, sketch_a, sketch_b):
    rows, depth, cols = volume.shape
    rank = sketch_a.shape[1]
    step = 64
    steps = rows // step
    outs = pl.pallas_call(
        first_sketch_kernel,
        grid=(steps,),
        in_specs=[
            pl.BlockSpec(memory_space=pltpu.SMEM),
            pl.BlockSpec((step, depth, cols), lambda g: (g, 0, 0)),
            pl.BlockSpec(sketch_a.shape, lambda g: (0, 0)),
            pl.BlockSpec(sketch_b.shape, lambda g: (0, 0)),
        ],
        out_specs=[pl.BlockSpec((rows // 2, rank), lambda g: (0, 0))] * 2
        + [pl.BlockSpec(memory_space=pltpu.HBM)] * len(SENT),
        out_shape=[jax.ShapeDtypeStruct((rows // 2, rank), jnp.float32)] * 2
        + [
            jax.ShapeDtypeStruct((rows // 2 if key[2] else rows, 8, cols), jnp.float32)
            for key in SENT
        ],
        scratch_shapes=[
            pltpu.VMEM((3 * cols, rank), jnp.bfloat16),
            pltpu.VMEM((step, rank), jnp.float32),
            pltpu.SemaphoreType.DMA((len(SENT),)),
        ],
        compiler_params=pltpu.CompilerParams(vmem_limit_bytes=VMEM_BYTES),
        cost_estimate=SMALL,
        name="first_sketch",
    )(place, volume, sketch_a, sketch_b)
    return outs[:2], dict(zip(SENT, outs[2:]))


def second_sketch_kernel(place, left_ref, right_ref, folded_ref, d_ref, *refs):
    kept_ref, given_ref, parts, total = refs
    rows, depth, _ = left_ref.shape

    @pl.when(pl.program_id(0) == 0)
    def _():
        parts[...] = left_parts(folded_ref[...])
        total[...] = jnp.zeros_like(total)

    weights = d_ref[...].T
    flats = [ref.reshape(rows * depth, LANES) for ref in (left_ref, right_ref)]
    for k in range(depth):
        cells = jnp.concatenate([flat[pl.ds(k, rows, stride=depth), :] for flat in flats], 1)
        mixed = dot_parts(parts[...], right_parts(cells))
        total[...] += mixed * weights[:, k : k + 1]

    @pl.when(pl.program_id(0) == pl.num_programs(0) - 1)
    def _():
        rows_ref = total
        rows_ref[...] = total[...].T
        half = kept_ref.shape[0]
        core = place[2]
        kept_ref[...] = rows_ref[pl.ds(pl.multiple_of(core * half, half), half), :]
        given_ref[...] = rows_ref[pl.ds(pl.multiple_of((1 - core) * half, half), half), :]


def second_sketch(place, volume, folded, sketch_d):
    rows, depth, cols = volume.shape
    rank = folded.shape[0]
    step = 8
    return pl.pallas_call(
        second_sketch_kernel,
        grid=(depth // step,),
        in_specs=[
            pl.BlockSpec(memory_space=pltpu.SMEM),
            pl.BlockSpec((rows, step, LANES), lambda g: (0, g, 0)),
            pl.BlockSpec((rows, step, LANES), lambda g: (0, g, 1)),
            pl.BlockSpec(folded.shape, lambda g: (0, 0)),
            pl.BlockSpec((step, rank), lambda g: (g, 0)),
        ],
        out_specs=[pl.BlockSpec((cols // 2, rank), lambda g: (0, 0))] * 2,
        out_shape=[jax.ShapeDtypeStruct((cols // 2, rank), jnp.float32)] * 2,
        scratch_shapes=[
            pltpu.VMEM((rank, 3 * rows), jnp.bfloat16),
            pltpu.VMEM((rank, cols), jnp.float32),
        ],
        compiler_params=pltpu.CompilerParams(vmem_limit_bytes=VMEM_BYTES),
        cost_estimate=SMALL,
        name="second_sketch",
    )(place, volume, volume, folded, sketch_d)


def factor_parts_kernel(place, inverse_ref, all_ref, x_ref, z_ref, by_x, by_z):
    rows = all_ref.shape[0] // 4
    for first in range(4):
        for second in range(4):
            block = lax.rem(place[0] + first, 4) * 64 + lax.rem(place[1] + second, 4) * 16
            moved = inverse_ref[pl.ds(pl.multiple_of(block, 16), 16), :]
            by_z[pl.ds(first * 64 + second * 16, 16), :] = moved
            by_x[pl.ds(second * 64 + first * 16, 16), :] = moved
    everything = all_ref[...]
    x_ref[...] = left_parts(dot_f32(by_z[...], everything[:rows], ((1,), (1,))))
    turned = dot_f32(by_x[...], everything, ((1,), (1,)))
    for s in range(4):
        z_ref[:, s * 3 * rows : (s + 1) * 3 * rows] = left_parts(turned[:, s * rows : (s + 1) * rows])


def factor_parts(place, inverse, all_rows):
    rank = all_rows.shape[1]
    rows = all_rows.shape[0] // 4
    return pl.pallas_call(
        factor_parts_kernel,
        in_specs=[pl.BlockSpec(memory_space=pltpu.SMEM)]
        + [pl.BlockSpec(memory_space=pltpu.VMEM)] * 2,
        out_shape=[
            jax.ShapeDtypeStruct((rank, 3 * rows), jnp.bfloat16),
            jax.ShapeDtypeStruct((rank, 12 * rows), jnp.bfloat16),
        ],
        scratch_shapes=[pltpu.VMEM((rank, rank), jnp.float32)] * 2,
        compiler_params=pltpu.CompilerParams(vmem_limit_bytes=VMEM_BYTES),
        cost_estimate=SMALL,
        name="factor_parts",
    )(place, inverse, all_rows)


def truncated_cell(q1_ref, source, flats, k):
    rows = flats[0].shape[0] // 8
    part = jnp.concatenate([flat[pl.ds(k, rows, stride=8), :] for flat in flats], 1)
    return dot_parts(q1_ref[:, source * 3 * rows : (source + 1) * 3 * rows], right_parts(part))


def lane_halves(held, at):
    rows = held.shape[1]
    return [held.at[2 * at + lane].reshape(rows * 8, LANES) for lane in range(2)]


def lane_copies(piece, held, at, rows, sems):
    return [
        pltpu.make_async_copy(
            piece.at[:, :, pl.ds(lane * LANES, LANES)], held.at[2 * at + lane, rows], sems.at[lane]
        )
        for lane in range(2)
    ]


def truncate_kernel(place, volume, *refs):
    one, three, q1_ref, total, held, sems = refs
    cells = pl.ds(pl.multiple_of(32 + place[0] * 8, 8), 8)
    everything = pl.ds(0, held.shape[1])
    copies = [
        lane_copies(piece, held, at, everything, sems.at[at])
        for at, piece in enumerate((volume.at[:, cells, :], one, three))
    ]
    for group in copies:
        for copy in group:
            copy.start()
    for at, source in enumerate((0, 1, 3)):
        for copy in copies[at]:
            copy.wait()
        flats = lane_halves(held, at)
        for k in range(8):
            product = truncated_cell(q1_ref, source, flats, k)
            total[k] = product if at == 0 else total[k] + product


def truncate(place, volume, pieces, q1):
    rows, _, cols = volume.shape
    return pl.pallas_call(
        truncate_kernel,
        in_specs=[pl.BlockSpec(memory_space=pltpu.SMEM)]
        + [pl.BlockSpec(memory_space=pltpu.HBM)]
        + [pl.BlockSpec(memory_space=pl.ANY)] * 2
        + [pl.BlockSpec(memory_space=pltpu.VMEM)],
        out_shape=jax.ShapeDtypeStruct((8, q1.shape[0], cols), jnp.float32),
        scratch_shapes=[
            pltpu.VMEM((6, rows, 8, LANES), jnp.float32),
            pltpu.SemaphoreType.DMA((3, 2)),
        ],
        compiler_params=pltpu.CompilerParams(vmem_limit_bytes=VMEM_BYTES),
        cost_estimate=SMALL,
        name="truncate",
    )(place, volume, *pieces, q1)


def finish_z_kernel(*refs):
    pieces, (t_ref, q1_ref, q2_ref) = refs[:2], refs[2:5]
    out_refs, (held, sems) = refs[5:9], refs[9:]
    half = held.shape[1] // 2
    copies = [
        copy
        for part in range(2)
        for copy in lane_copies(pieces[part], held, 0, pl.ds(part * half, half), sems.at[part])
    ]
    for copy in copies:
        copy.start()
    weights = right_parts(q2_ref[...])
    for copy in copies:
        copy.wait()
    flats = lane_halves(held, 0)
    share = out_refs[0].shape[1]
    for k in range(8):
        total = t_ref[k] + truncated_cell(q1_ref, 2, flats, k)
        product = dot_parts(left_parts(total), weights)
        for b in range(4):
            out_refs[b][k] = product[b * share : (b + 1) * share]


def finish_z(pieces, truncated, q1, q2):
    rows = pieces[0].shape[0] * 2
    rank_first, rank_second = q1.shape[0], q2.shape[1]
    block = jax.ShapeDtypeStruct((8, rank_first // 4, rank_second), jnp.float32)
    return pl.pallas_call(
        finish_z_kernel,
        in_specs=[pl.BlockSpec(memory_space=pl.ANY)] * 2
        + [pl.BlockSpec(memory_space=pltpu.VMEM)] * 3,
        out_shape=[block] * 4,
        scratch_shapes=[
            pltpu.VMEM((2, rows, 8, LANES), jnp.float32),
            pltpu.SemaphoreType.DMA((2, 2)),
        ],
        compiler_params=pltpu.CompilerParams(vmem_limit_bytes=VMEM_BYTES),
        cost_estimate=SMALL,
        name="finish_z",
    )(*pieces, truncated, q1, q2)


def finish_x_kernel(place, volume, *refs):
    (one, two, two_b, three, q1_ref, q2_ref), out_refs = refs[:6], refs[6:10]
    held, spread, weights, sems = refs[10:]
    rows = held.shape[2] * 2
    half = rows // 2
    cells = pl.ds(pl.multiple_of(place[1] * 8, 8), 8)
    copies = [[], []]
    for part in range(2):
        copies[part].append(
            pltpu.make_async_copy(
                volume.at[pl.ds(part * half, half), cells], held.at[0, part], sems.at[part]
            )
        )
        rows_of = pl.ds(part * half, half)
        pieces = (one.at[rows_of], (two, two_b)[part], three.at[rows_of])
        for source, piece in enumerate(pieces):
            copies[part].append(
                pltpu.make_async_copy(
                    piece, held.at[1 + source, part], sems.at[2 + 2 * source + part]
                )
            )
    for copy in copies[0] + copies[1]:
        copy.start()
    cols = held.shape[4]
    for s in range(4):
        weights[s * 3 * cols : (s + 1) * 3 * cols, :] = right_parts(
            q2_ref[s * cols : (s + 1) * cols, :]
        )
    chunk = 256
    for part in range(2):
        for copy in copies[part]:
            copy.wait()
        for top in range(0, half * 8, chunk):
            lhs = jnp.concatenate(
                [
                    left_parts(held.at[s, part].reshape(half * 8, cols)[top : top + chunk, :])
                    for s in range(4)
                ],
                1,
            )
            mapped = dot_parts(lhs, weights[...])
            for lane in range(2):
                spread[lane, pl.ds(part * half * 8 + top, chunk), :] = mapped[
                    :, lane * LANES : (lane + 1) * LANES
                ]
    share = out_refs[0].shape[1]
    for k in range(8):
        mapped = jnp.concatenate(
            [spread.at[lane][pl.ds(k, rows, stride=8), :] for lane in range(2)], 1
        )
        product = dot_parts(q1_ref[...], right_parts(mapped))
        for b in range(4):
            out_refs[b][k] = product[b * share : (b + 1) * share]


def finish_x(place, volume, pieces, q1, q2):
    rows, _, cols = volume.shape
    rank_first, rank_second = q1.shape[0], q2.shape[1]
    block = jax.ShapeDtypeStruct((8, rank_first // 4, rank_second), jnp.float32)
    return pl.pallas_call(
        finish_x_kernel,
        in_specs=[pl.BlockSpec(memory_space=pltpu.SMEM)]
        + [pl.BlockSpec(memory_space=pltpu.HBM)]
        + [pl.BlockSpec(memory_space=pl.ANY)] * 4
        + [pl.BlockSpec(memory_space=pltpu.VMEM)] * 2,
        out_shape=[block] * 4,
        scratch_shapes=[
            pltpu.VMEM((4, 2, rows // 2, 8, cols), jnp.float32),
            pltpu.VMEM((2, rows * 8, LANES), jnp.float32),
            pltpu.VMEM((12 * cols, rank_second), jnp.bfloat16),
            pltpu.SemaphoreType.DMA((8,)),
        ],
        compiler_params=pltpu.CompilerParams(vmem_limit_bytes=VMEM_BYTES),
        cost_estimate=SMALL,
        name="finish_x",
    )(place, volume, *pieces, q1, q2)


def assemble_kernel(place, *refs):
    pieces, out_ref = refs[:8], refs[8]
    for b in range(4):
        x_cells = pl.ds(pl.multiple_of(lax.rem(place[1] + 4 - b, 4) * 8, 8), 8)
        z_cells = pl.ds(pl.multiple_of(32 + lax.rem(place[0] + 4 - b, 4) * 8, 8), 8)
        out_ref[:, x_cells, :] = jnp.swapaxes(pieces[b][...], 0, 1)
        out_ref[:, z_cells, :] = jnp.swapaxes(pieces[4 + b][...], 0, 1)


def assemble(place, x_pieces, z_pieces):
    _, rows, cols = x_pieces[0].shape
    return pl.pallas_call(
        assemble_kernel,
        in_specs=[pl.BlockSpec(memory_space=pltpu.SMEM)]
        + [pl.BlockSpec(memory_space=pltpu.VMEM)] * 8,
        out_shape=jax.ShapeDtypeStruct((rows, 64, cols), jnp.float32),
        compiler_params=pltpu.CompilerParams(vmem_limit_bytes=VMEM_BYTES),
        cost_estimate=SMALL,
        name="assemble",
    )(place, *x_pieces, *z_pieces)


def swap_cores(array):
    return lax.ppermute(array, "gz", [(i, i ^ 1) for i in range(lax.axis_size("gz"))])


def shifted(array, axis, step):
    size = lax.axis_size(axis)
    if axis == "gz":
        chips = size // 2
        pairs = [(i, ((i // 2 + step) % chips) * 2 + i % 2) for i in range(size)]
    else:
        pairs = [(i, (i + step) % size) for i in range(size)]
    return lax.ppermute(array, axis, pairs)


def sum_along(array, axis, beside=()):
    one, three, two = (shifted(array, axis, step) for step in (1, 3, 2))
    one, three, two, *beside = lax.optimization_barrier((one, three, two, *beside))
    return (array + two) + (one + three), beside


def behind(array, token):
    return lax.optimization_barrier((array, token))[0]


def gathered(mine, axis):
    received = [shifted(mine, axis, step) for step in (1, 2, 3)]
    shares = jnp.stack([mine, *received])
    return (shares, swap_cores(shares)), received


def scatter_sum(blocks, axis):
    one, three, two = (shifted(blocks[step], axis, step) for step in (1, 3, 2))
    return (blocks[0] + two) + (one + three)


def spread_rows(total, axis):
    share = total.shape[1] // 4
    blocks = [total[:, b * share : (b + 1) * share] for b in range(4)]
    return [blocks[0]] + [shifted(blocks[b], axis, b) for b in (1, 2, 3)]


def on_device(volume, sketch_a, sketch_b, sketch_c, sketch_d):
    place = jnp.stack(
        [lax.axis_index("gx"), lax.axis_index("gy"), lax.rem(lax.axis_index("gz"), 2)]
    ).astype(jnp.int32)
    axes = ("gy", "gx")
    moved = {}

    def send(token, kind, shift, second=False):
        piece = sent[kind, shift, second]
        moved[kind, shift, second] = shifted(behind(piece, token), axes[kind], shift)

    def send_first(kind):
        target = lax.rem(lax.axis_index(axes[kind]) + 2, 4) * 8 + 32 * kind
        rows, _, cols = volume.shape
        piece = lax.dynamic_slice(volume, (0, target, 0), (rows // 2, 8, cols))
        moved[kind, 2, False] = shifted(piece, axes[kind], 2)

    def arrived(array, *keys):
        held = lax.optimization_barrier((array, *(moved[key] for key in keys)))
        moved.update(zip(keys, held[1:]))
        return held[0]

    send_first(0)
    send_first(1)
    (kept, given), sent = first_sketch(place, volume, sketch_a, sketch_b)
    summed, _ = sum_along(kept + swap_cores(given), "gz")
    summed, _ = sum_along(arrived(summed, (0, 2, False), (1, 2, False)), "gy")
    send(summed, 0, 1)
    send(summed, 0, 3)
    shares, received = gathered(summed, "gx")
    send(received, 1, 1)
    send(received, 1, 3)
    q_first, folded, inverse, all_first = first_orthonormal(place, shares, sketch_c)

    kept, given = second_sketch(place, volume, folded, sketch_d)
    summed = arrived(kept + swap_cores(given), (0, 1, False), (0, 3, False))
    q1 = factor_parts(place, behind(inverse, summed), all_first)
    summed, (q1_x, q1_z) = sum_along(summed, "gz", q1)
    summed = arrived(summed, (1, 1, False), (1, 3, False))
    truncated = truncate(place, volume, [moved[1, 1, False], moved[1, 3, False]], behind(q1_z, summed))
    summed, (truncated,) = sum_along(summed, "gx", [truncated])
    shares, received = gathered(summed, "gy")
    send(received[0], 1, 2, True)
    send(shares[1], 0, 2, True)
    q_second, q2 = second_orthonormal(place, shares)

    z_blocks = finish_z([moved[1, 2, False], moved[1, 2, True]], truncated, q1_z, q_second)
    q2, z_first = lax.optimization_barrier((q2, z_blocks[0]))
    z_blocks = [z_first, *z_blocks[1:]]
    ready = [moved[0, 1, False], moved[0, 2, False], moved[0, 2, True], moved[0, 3, False]]
    x_blocks = finish_x(place, volume, ready, q1_x, q2)
    z_total = scatter_sum(z_blocks, "gy")
    x_total = scatter_sum(x_blocks, "gx")
    z_pieces = spread_rows(z_total, "gx")
    core_out = assemble(place, spread_rows(x_total, "gy"), z_pieces)
    return (q_first, q_second, core_out)


def solution(mesh):
    placed = (P("gx", "gz", "gy"), P("gy", None), P("gz", None), P(), P("gz", None))
    return jax.shard_map(
        on_device,
        mesh=mesh,
        in_specs=placed,
        out_specs=(P("gx", None), P("gy", None), P(("gx", "gy"), "gz", None)),
        check_vma=False,
    )
```

```python
import functools

import jax
import jax.numpy as jnp
from jax import lax
from jax.experimental import pallas as pl
from jax.experimental.pallas import tpu as pltpu
from jax.sharding import PartitionSpec as P

HIGHEST = lax.Precision.HIGHEST
LANES = 128
PANEL = 32
GROUP = 16
VMEM_BYTES = 28 * 2**20
VMEM_BYTES_SKETCH = 52 * 2**20
SMALL = pl.CostEstimate(flops=2**20, bytes_accessed=2**16, transcendentals=0)
FIRST_ROWS = 160
STEPS = 4
SENT = [(kind, shift, 0, 256) for kind in (0, 1) for shift in (0, 1, 3)]
SENT += [(0, 2, FIRST_ROWS, 96), (1, 2, FIRST_ROWS, 64), (1, 2, 224, 32)]


def dot_f32(a, b, contract):
    return lax.dot_general(
        a, b, (contract, ((), ())), precision=HIGHEST, preferred_element_type=jnp.float32
    )


def factor_inverse(work, inverse):
    n = work.shape[0]
    halves = n // LANES
    rows_at = lax.broadcasted_iota(jnp.int32, (n, n), 0)
    columns_at = lax.broadcasted_iota(jnp.int32, (n, n), 1)
    inverse[...] = jnp.where(rows_at == columns_at, 1.0, 0.0)
    row = lax.broadcasted_iota(jnp.int32, (PANEL, LANES), 0)
    for top in range(0, n, PANEL):
        half = top // LANES
        left = half * LANES
        bottom = top + PANEL
        tiles = [work[top:bottom, t * LANES : (t + 1) * LANES] for t in range(half, halves)]
        tiles += [inverse[top:bottom, t * LANES : (t + 1) * LANES] for t in range(half + 1)]
        pivots = jnp.ones((PANEL, LANES), jnp.float32)
        for start in range(0, PANEL, GROUP):
            first = top - left + start
            columns = [
                jnp.broadcast_to(tiles[0][:, first + m : first + m + 1], (PANEL, LANES))
                for m in range(GROUP)
            ]
            for m in range(GROUP):
                at = start + m
                pivot = columns[m][at : at + 1, :]
                pivots = jnp.where(row == at, pivot, pivots)
                factor = jnp.where(row > at, columns[m] * (1.0 / pivot), 0.0)
                for later in range(m + 1, GROUP):
                    columns[later] = columns[later] - factor * columns[later][at : at + 1, :]
                tiles = [tile - factor * tile[at : at + 1, :] for tile in tiles]
        scale = lax.rsqrt(pivots)
        tiles = [tile * scale for tile in tiles]
        kept = halves - half
        for t in range(half + 1):
            inverse[top:bottom, t * LANES : (t + 1) * LANES] = tiles[kept + t]
        if bottom < n:
            upper = jnp.concatenate(tiles[:kept], 1)
            solved = jnp.concatenate(tiles[kept:], 1)
            lower = upper.T[bottom - left :, :]
            work[bottom:, left:] = work[bottom:, left:] - dot_f32(lower, upper, ((1,), (0,)))
            inverse[bottom:, : left + LANES] = inverse[bottom:, : left + LANES] - dot_f32(
                lower, solved, ((1,), (0,))
            )


def split(x):
    high = x.astype(jnp.bfloat16)
    return high, (x - high.astype(jnp.float32)).astype(jnp.bfloat16)


def left_parts(x):
    high, low = split(x)
    return jnp.concatenate([high, high, low], 1)


def right_parts(x):
    high, low = split(x)
    return jnp.concatenate([high, low, high], 0)


def dot_parts(a, b):
    return jnp.dot(a, b, preferred_element_type=jnp.float32)


def place_rows(core, shares_ref, others_ref, all_ref):
    half = shares_ref.shape[1]
    for at in range(4):
        top = at * 2 * half
        mine = pl.multiple_of(top + core * half, half)
        other = pl.multiple_of(top + (1 - core) * half, half)
        all_ref[pl.ds(mine, half), :] = shares_ref[at]
        all_ref[pl.ds(other, half), :] = others_ref[at]


def first_orthonormal_kernel(place, *refs):
    shares, others, c_ref, q_ref, folded_ref, inverse_ref, all_ref, work = refs
    place_rows(place[2], shares, others, all_ref)
    rows = all_ref[...]
    n = rows.shape[1]
    work[...] = dot_f32(rows, rows, ((0,), (0,)))
    factor_inverse(work, inverse_ref)
    q = dot_f32(rows[:n], inverse_ref[...], ((1,), (1,)))
    q_ref[...] = q
    folded_ref[...] = dot_f32(c_ref[...], q, ((0,), (1,)))


def first_orthonormal(place, shares, sketch_c):
    _, half, n = shares[0].shape
    square = jax.ShapeDtypeStruct((n, n), jnp.float32)
    return pl.pallas_call(
        first_orthonormal_kernel,
        in_specs=[pl.BlockSpec(memory_space=pltpu.SMEM)]
        + [pl.BlockSpec(memory_space=pltpu.VMEM)] * 3,
        out_shape=[square] * 3 + [jax.ShapeDtypeStruct((8 * half, n), jnp.float32)],
        scratch_shapes=[pltpu.VMEM((n, n), jnp.float32)],
        compiler_params=pltpu.CompilerParams(vmem_limit_bytes=VMEM_BYTES_SKETCH),
        cost_estimate=SMALL,
        name="first_orthonormal",
    )(place, *shares, sketch_c)


def second_orthonormal_kernel(place, *refs):
    shares, others, q_ref, q_all_ref, all_ref, work, inverse = refs
    place_rows(place[2], shares, others, all_ref)
    rows = all_ref[...]
    n = rows.shape[1]
    work[...] = dot_f32(rows, rows, ((0,), (0,)))
    factor_inverse(work, inverse)
    q = dot_f32(rows, inverse[...], ((1,), (1,)))
    q_ref[...] = q[:n]
    q_all_ref[...] = q


def second_orthonormal(place, shares):
    _, half, n = shares[0].shape
    return pl.pallas_call(
        second_orthonormal_kernel,
        in_specs=[pl.BlockSpec(memory_space=pltpu.SMEM)]
        + [pl.BlockSpec(memory_space=pltpu.VMEM)] * 2,
        out_shape=[
            jax.ShapeDtypeStruct((n, n), jnp.float32),
            jax.ShapeDtypeStruct((8 * half, n), jnp.float32),
        ],
        scratch_shapes=[
            pltpu.VMEM((8 * half, n), jnp.float32),
            pltpu.VMEM((n, n), jnp.float32),
            pltpu.VMEM((n, n), jnp.float32),
        ],
        compiler_params=pltpu.CompilerParams(vmem_limit_bytes=VMEM_BYTES),
        cost_estimate=SMALL,
        name="second_orthonormal",
    )(place, *shares)


def first_sketch_kernel(place, v_ref, a_ref, b_ref, kept_ref, given_ref, *refs):
    sent, (parts, rows_ref, sems) = refs[: len(SENT)], refs[len(SENT) :]
    rows, depth, cols = v_ref.shape
    step = pl.program_id(0)
    steps = STEPS

    @pl.when(step == 0)
    def _():
        parts[...] = right_parts(a_ref[...])

    half_steps = steps // 2
    at = pl.ds(pl.multiple_of(lax.rem(step, half_steps) * rows, rows), rows)

    def copies_out(g):
        copies = []
        for key, (kind, shift, first, count) in enumerate(SENT):
            start, stop = max(first, g * rows), min(first + count, (g + 1) * rows)
            if start < stop:
                target = lax.rem(place[1 - kind] + shift, 4) * 8 + 32 * kind
                cells = pl.ds(pl.multiple_of(target, 8), 8)
                copies.append(
                    pltpu.make_async_copy(
                        v_ref.at[pl.ds(start - g * rows, stop - start), cells, :],
                        sent[key].at[pl.ds(start - first, stop - start)],
                        sems.at[key],
                    )
                )
        return copies

    for g in range(STEPS):

        @pl.when(step == g)
        def _():
            for copy in copies_out(g):
                copy.start()

    flat = v_ref.reshape(rows * depth, cols)
    weights = b_ref[...]
    for top in range(0, rows, 8):
        spread = dot_parts(left_parts(flat[top * depth : (top + 8) * depth, :]), parts[...])
        rows_ref[top : top + 8, :] = jnp.sum(spread.reshape(8, depth, -1) * weights[None], axis=1)

    @pl.when(step // half_steps == place[2])
    def _():
        kept_ref[at, :] = rows_ref[...]

    @pl.when(step // half_steps != place[2])
    def _():
        given_ref[at, :] = rows_ref[...]

    for g in range(STEPS):

        @pl.when(step == g)
        def _():
            for copy in copies_out(g):
                copy.wait()


def first_sketch(place, volume, sketch_a, sketch_b):
    rows, depth, cols = volume.shape
    rank = sketch_a.shape[1]
    step = rows // STEPS
    outs = pl.pallas_call(
        first_sketch_kernel,
        grid=(STEPS,),
        in_specs=[
            pl.BlockSpec(memory_space=pltpu.SMEM),
            pl.BlockSpec((step, depth, cols), lambda g: (g, 0, 0)),
            pl.BlockSpec(sketch_a.shape, lambda g: (0, 0)),
            pl.BlockSpec(sketch_b.shape, lambda g: (0, 0)),
        ],
        out_specs=[pl.BlockSpec((rows // 2, rank), lambda g: (0, 0))] * 2
        + [pl.BlockSpec(memory_space=pl.ANY)] * len(SENT),
        out_shape=[jax.ShapeDtypeStruct((rows // 2, rank), jnp.float32)] * 2
        + [
            jax.ShapeDtypeStruct((count, 8, cols), jnp.float32) for _, _, _, count in SENT
        ],
        scratch_shapes=[
            pltpu.VMEM((3 * cols, rank), jnp.bfloat16),
            pltpu.VMEM((step, rank), jnp.float32),
            pltpu.SemaphoreType.DMA((len(SENT),)),
        ],
        compiler_params=pltpu.CompilerParams(vmem_limit_bytes=VMEM_BYTES_SKETCH),
        cost_estimate=SMALL,
        name="first_sketch",
    )(place, volume, sketch_a, sketch_b)
    return outs[:2], {key[:3]: out for key, out in zip(SENT, outs[2:])}


def second_sketch_kernel(place, left_ref, right_ref, folded_ref, d_ref, *refs):
    kept_ref, given_ref, parts, total = refs
    rows, depth, _ = left_ref.shape

    @pl.when(pl.program_id(0) == 0)
    def _():
        parts[...] = left_parts(folded_ref[...])
        total[...] = jnp.zeros_like(total)

    weights = d_ref[...].T
    flats = [ref.reshape(rows * depth, LANES) for ref in (left_ref, right_ref)]
    for k in range(depth):
        cells = jnp.concatenate([flat[pl.ds(k, rows, stride=depth), :] for flat in flats], 1)
        mixed = dot_parts(parts[...], right_parts(cells))
        total[...] += mixed * weights[:, k : k + 1]

    @pl.when(pl.program_id(0) == pl.num_programs(0) - 1)
    def _():
        rows_ref = total
        rows_ref[...] = total[...].T
        half = kept_ref.shape[0]
        core = place[2]
        kept_ref[...] = rows_ref[pl.ds(pl.multiple_of(core * half, half), half), :]
        given_ref[...] = rows_ref[pl.ds(pl.multiple_of((1 - core) * half, half), half), :]


def second_sketch(place, volume, folded, sketch_d):
    rows, depth, cols = volume.shape
    rank = folded.shape[0]
    step = 8
    return pl.pallas_call(
        second_sketch_kernel,
        grid=(depth // step,),
        in_specs=[
            pl.BlockSpec(memory_space=pltpu.SMEM),
            pl.BlockSpec((rows, step, LANES), lambda g: (0, g, 0)),
            pl.BlockSpec((rows, step, LANES), lambda g: (0, g, 1)),
            pl.BlockSpec(folded.shape, lambda g: (0, 0)),
            pl.BlockSpec((step, rank), lambda g: (g, 0)),
        ],
        out_specs=[pl.BlockSpec((cols // 2, rank), lambda g: (0, 0))] * 2,
        out_shape=[jax.ShapeDtypeStruct((cols // 2, rank), jnp.float32)] * 2,
        scratch_shapes=[
            pltpu.VMEM((rank, 3 * rows), jnp.bfloat16),
            pltpu.VMEM((rank, cols), jnp.float32),
        ],
        compiler_params=pltpu.CompilerParams(vmem_limit_bytes=VMEM_BYTES_SKETCH),
        cost_estimate=SMALL,
        name="second_sketch",
    )(place, volume, volume, folded, sketch_d)


def factor_parts_kernel(place, inverse_ref, all_ref, x_ref, z_ref, by_x, by_z):
    rows = all_ref.shape[0] // 4
    for first in range(4):
        for second in range(4):
            block = lax.rem(place[0] + first, 4) * 64 + lax.rem(place[1] + second, 4) * 16
            moved = inverse_ref[pl.ds(pl.multiple_of(block, 16), 16), :]
            by_z[pl.ds(first * 64 + second * 16, 16), :] = moved
            by_x[pl.ds(second * 64 + first * 16, 16), :] = moved
    everything = all_ref[...]
    x_ref[...] = left_parts(dot_f32(by_z[...], everything[:rows], ((1,), (1,))))
    turned = dot_f32(by_x[...], everything, ((1,), (1,)))
    for s in range(4):
        z_ref[:, s * 3 * rows : (s + 1) * 3 * rows] = left_parts(turned[:, s * rows : (s + 1) * rows])


def factor_parts(place, inverse, all_rows):
    rank = all_rows.shape[1]
    rows = all_rows.shape[0] // 4
    return pl.pallas_call(
        factor_parts_kernel,
        in_specs=[pl.BlockSpec(memory_space=pltpu.SMEM)]
        + [pl.BlockSpec(memory_space=pltpu.VMEM)] * 2,
        out_shape=[
            jax.ShapeDtypeStruct((rank, 3 * rows), jnp.bfloat16),
            jax.ShapeDtypeStruct((rank, 12 * rows), jnp.bfloat16),
        ],
        scratch_shapes=[pltpu.VMEM((rank, rank), jnp.float32)] * 2,
        compiler_params=pltpu.CompilerParams(vmem_limit_bytes=VMEM_BYTES),
        cost_estimate=SMALL,
        name="factor_parts",
    )(place, inverse, all_rows)


def truncated_cell(q1_ref, source, flats, k):
    rows = flats[0].shape[0] // 8
    part = jnp.concatenate([flat[pl.ds(k, rows, stride=8), :] for flat in flats], 1)
    return dot_parts(q1_ref[:, source * 3 * rows : (source + 1) * 3 * rows], right_parts(part))


def lane_halves(held, at):
    rows = held.shape[1]
    return [held.at[2 * at + lane].reshape(rows * 8, LANES) for lane in range(2)]


def lane_copies(piece, held, at, rows, sems):
    return [
        pltpu.make_async_copy(
            piece.at[:, :, pl.ds(lane * LANES, LANES)], held.at[2 * at + lane, rows], sems.at[lane]
        )
        for lane in range(2)
    ]


def truncate_kernel(own, one, three, q1_ref, total, held, sems):
    everything = pl.ds(0, held.shape[1])
    copies = [
        lane_copies(piece, held, at, everything, sems.at[at])
        for at, piece in enumerate((own, one, three))
    ]
    for group in copies:
        for copy in group:
            copy.start()
    for at, source in enumerate((0, 1, 3)):
        for copy in copies[at]:
            copy.wait()
        flats = lane_halves(held, at)
        for k in range(8):
            product = truncated_cell(q1_ref, source, flats, k)
            total[k] = product if at == 0 else total[k] + product


def truncate(pieces, q1):
    rows, _, cols = pieces[0].shape
    return pl.pallas_call(
        truncate_kernel,
        in_specs=[pl.BlockSpec(memory_space=pl.ANY)] * 3
        + [pl.BlockSpec(memory_space=pltpu.VMEM)],
        out_shape=jax.ShapeDtypeStruct((8, q1.shape[0], cols), jnp.float32),
        scratch_shapes=[
            pltpu.VMEM((6, rows, 8, LANES), jnp.float32),
            pltpu.SemaphoreType.DMA((3, 2)),
        ],
        compiler_params=pltpu.CompilerParams(vmem_limit_bytes=VMEM_BYTES),
        cost_estimate=SMALL,
        name="truncate",
    )(*pieces, q1)


def finish_z_kernel(*refs):
    pieces, (t_ref, q1_ref, q2_ref) = refs[:3], refs[3:6]
    out_refs, (held, sems) = refs[6:10], refs[10:]
    copies = []
    first = 0
    for at, piece in enumerate(pieces):
        rows_at = pl.ds(first, piece.shape[0])
        copies += lane_copies(piece, held, 0, rows_at, sems.at[at])
        first += piece.shape[0]
    for copy in copies:
        copy.start()
    weights = right_parts(q2_ref[...])
    for copy in copies:
        copy.wait()
    flats = lane_halves(held, 0)
    share = out_refs[0].shape[1]
    for k in range(8):
        total = t_ref[k] + truncated_cell(q1_ref, 2, flats, k)
        product = dot_parts(left_parts(total), weights)
        for b in range(4):
            out_refs[b][k] = product[b * share : (b + 1) * share]


def finish_z(pieces, truncated, q1, q2):
    rows = sum(piece.shape[0] for piece in pieces)
    rank_first, rank_second = q1.shape[0], q2.shape[1]
    block = jax.ShapeDtypeStruct((8, rank_first // 4, rank_second), jnp.float32)
    return pl.pallas_call(
        finish_z_kernel,
        in_specs=[pl.BlockSpec(memory_space=pl.ANY)] * 3
        + [pl.BlockSpec(memory_space=pltpu.VMEM)] * 3,
        out_shape=[block] * 4,
        scratch_shapes=[
            pltpu.VMEM((2, rows, 8, LANES), jnp.float32),
            pltpu.SemaphoreType.DMA((3, 2)),
        ],
        compiler_params=pltpu.CompilerParams(vmem_limit_bytes=VMEM_BYTES),
        cost_estimate=SMALL,
        name="finish_z",
    )(*pieces, truncated, q1, q2)


def finish_x_kernel(*refs):
    (own, one, two, two_b, three, q1_ref, q2_ref), out_refs = refs[:7], refs[7:11]
    held, spread, weights, sems = refs[11:]
    rows = held.shape[2] * 2
    half = rows // 2
    copies = [[], []]
    cut = two.shape[0] - half
    parts = [(0, 0, own.at[pl.ds(0, half)], 0), (0, 1, one.at[pl.ds(0, half)], 0)]
    parts += [(0, 2, two.at[pl.ds(0, half)], 0), (0, 3, three.at[pl.ds(0, half)], 0)]
    parts += [(1, 0, own.at[pl.ds(half, half)], 0), (1, 1, one.at[pl.ds(half, half)], 0)]
    parts += [(1, 3, three.at[pl.ds(half, half)], 0), (1, 2, two.at[pl.ds(half, cut)], 0)]
    parts += [(1, 2, two_b, cut)]
    for at, (part, source, piece, first) in enumerate(parts):
        to = held.at[source, part, pl.ds(first, piece.shape[0])]
        copies[part].append(pltpu.make_async_copy(piece, to, sems.at[at]))
    for copy in copies[0] + copies[1]:
        copy.start()
    cols = held.shape[4]
    for s in range(4):
        weights[s * 3 * cols : (s + 1) * 3 * cols, :] = right_parts(
            q2_ref[s * cols : (s + 1) * cols, :]
        )
    chunk = 256
    for part in range(2):
        for copy in copies[part]:
            copy.wait()
        for top in range(0, half * 8, chunk):
            lhs = jnp.concatenate(
                [
                    left_parts(held.at[s, part].reshape(half * 8, cols)[top : top + chunk, :])
                    for s in range(4)
                ],
                1,
            )
            mapped = dot_parts(lhs, weights[...])
            for lane in range(2):
                spread[lane, pl.ds(part * half * 8 + top, chunk), :] = mapped[
                    :, lane * LANES : (lane + 1) * LANES
                ]
    share = out_refs[0].shape[1]
    for k in range(8):
        mapped = jnp.concatenate(
            [spread.at[lane][pl.ds(k, rows, stride=8), :] for lane in range(2)], 1
        )
        product = dot_parts(q1_ref[...], right_parts(mapped))
        for b in range(4):
            out_refs[b][k] = product[b * share : (b + 1) * share]


def finish_x(pieces, q1, q2):
    rows, _, cols = pieces[0].shape
    rank_first, rank_second = q1.shape[0], q2.shape[1]
    block = jax.ShapeDtypeStruct((8, rank_first // 4, rank_second), jnp.float32)
    return pl.pallas_call(
        finish_x_kernel,
        in_specs=[pl.BlockSpec(memory_space=pl.ANY)] * 5
        + [pl.BlockSpec(memory_space=pltpu.VMEM)] * 2,
        out_shape=[block] * 4,
        scratch_shapes=[
            pltpu.VMEM((4, 2, rows // 2, 8, cols), jnp.float32),
            pltpu.VMEM((2, rows * 8, LANES), jnp.float32),
            pltpu.VMEM((12 * cols, rank_second), jnp.bfloat16),
            pltpu.SemaphoreType.DMA((9,)),
        ],
        compiler_params=pltpu.CompilerParams(vmem_limit_bytes=VMEM_BYTES),
        cost_estimate=SMALL,
        name="finish_x",
    )(*pieces, q1, q2)


def assemble_kernel(place, *refs):
    pieces, out_ref = refs[:8], refs[8]
    for b in range(4):
        x_cells = pl.ds(pl.multiple_of(lax.rem(place[1] + 4 - b, 4) * 8, 8), 8)
        z_cells = pl.ds(pl.multiple_of(32 + lax.rem(place[0] + 4 - b, 4) * 8, 8), 8)
        out_ref[:, x_cells, :] = jnp.swapaxes(pieces[b][...], 0, 1)
        out_ref[:, z_cells, :] = jnp.swapaxes(pieces[4 + b][...], 0, 1)


def assemble(place, x_pieces, z_pieces):
    _, rows, cols = x_pieces[0].shape
    return pl.pallas_call(
        assemble_kernel,
        in_specs=[pl.BlockSpec(memory_space=pltpu.SMEM)]
        + [pl.BlockSpec(memory_space=pltpu.VMEM)] * 8,
        out_shape=jax.ShapeDtypeStruct((rows, 64, cols), jnp.float32),
        compiler_params=pltpu.CompilerParams(vmem_limit_bytes=VMEM_BYTES),
        cost_estimate=SMALL,
        name="assemble",
    )(place, *x_pieces, *z_pieces)


def swap_cores(array):
    return lax.ppermute(array, "gz", [(i, i ^ 1) for i in range(lax.axis_size("gz"))])


def shifted(array, axis, step):
    size = lax.axis_size(axis)
    if axis == "gz":
        chips = size // 2
        pairs = [(i, ((i // 2 + step) % chips) * 2 + i % 2) for i in range(size)]
    else:
        pairs = [(i, (i + step) % size) for i in range(size)]
    return lax.ppermute(array, axis, pairs)


def sum_along(array, axis, beside=()):
    one, three, two = (shifted(array, axis, step) for step in (1, 3, 2))
    one, three, two, *beside = lax.optimization_barrier((one, three, two, *beside))
    return (array + two) + (one + three), beside


def behind(array, token):
    return lax.optimization_barrier((array, token))[0]


def gathered(mine, axis):
    received = [shifted(mine, axis, step) for step in (1, 2, 3)]
    shares = jnp.stack([mine, *received])
    return (shares, swap_cores(shares)), received


def scatter_sum(blocks, axis):
    one, three, two = (shifted(blocks[step], axis, step) for step in (1, 3, 2))
    return (blocks[0] + two) + (one + three)


def spread_rows(total, axis):
    share = total.shape[1] // 4
    blocks = [total[:, b * share : (b + 1) * share] for b in range(4)]
    return [blocks[0]] + [shifted(blocks[b], axis, b) for b in (1, 2, 3)]


def on_device(volume, sketch_a, sketch_b, sketch_c, sketch_d):
    place = jnp.stack(
        [lax.axis_index("gx"), lax.axis_index("gy"), lax.rem(lax.axis_index("gz"), 2)]
    ).astype(jnp.int32)
    axes = ("gy", "gx")
    moved = {}

    def send(token, kind, shift, first=0):
        piece = sent[kind, shift, first]
        moved[kind, shift, first] = shifted(behind(piece, token), axes[kind], shift)

    def send_first(kind):
        target = lax.rem(lax.axis_index(axes[kind]) + 2, 4) * 8 + 32 * kind
        piece = lax.dynamic_slice(volume, (0, target, 0), (FIRST_ROWS, 8, volume.shape[2]))
        moved[kind, 2, 0] = shifted(piece, axes[kind], 2)

    def arrived(array, *keys):
        held = lax.optimization_barrier((array, *(moved[key] for key in keys)))
        moved.update(zip(keys, held[1:]))
        return held[0]

    send_first(0)
    send_first(1)
    (kept, given), sent = first_sketch(place, volume, sketch_a, sketch_b)
    summed, _ = sum_along(kept + swap_cores(given), "gz")
    summed = arrived(summed, (0, 2, 0), (1, 2, 0))
    send(summed, 1, 2, FIRST_ROWS)
    summed, _ = sum_along(summed, "gy")
    send(summed, 0, 1)
    send(summed, 0, 3)
    shares, received = gathered(arrived(summed, (1, 2, FIRST_ROWS)), "gx")
    send(received, 1, 1)
    send(received, 1, 3)
    q_first, folded, inverse, all_first = first_orthonormal(place, shares, sketch_c)

    kept, given = second_sketch(place, volume, folded, sketch_d)
    summed = arrived(kept + swap_cores(given), (0, 1, 0), (0, 3, 0))
    q1 = factor_parts(place, behind(inverse, summed), all_first)
    summed, (q1_x, q1_z) = sum_along(summed, "gz", q1)
    summed = arrived(summed, (1, 1, 0), (1, 3, 0))
    ready = [sent[1, 0, 0], moved[1, 1, 0], moved[1, 3, 0]]
    truncated = truncate(ready, behind(q1_z, summed))
    summed, (truncated,) = sum_along(summed, "gx", [truncated])
    send(summed, 1, 2, 224)
    shares, _ = gathered(summed, "gy")
    send(shares[1], 0, 2, FIRST_ROWS)
    q_second, q2 = second_orthonormal(place, shares)

    ready = [moved[1, 2, 0], moved[1, 2, FIRST_ROWS], moved[1, 2, 224]]
    z_blocks = finish_z(ready, truncated, q1_z, q_second)
    q2, z_first = lax.optimization_barrier((q2, z_blocks[0]))
    z_blocks = [z_first, *z_blocks[1:]]
    ready = [sent[0, 0, 0]]
    ready += [moved[0, 1, 0], moved[0, 2, 0], moved[0, 2, FIRST_ROWS], moved[0, 3, 0]]
    x_blocks = finish_x(ready, q1_x, q2)
    z_total = scatter_sum(z_blocks, "gy")
    x_total = scatter_sum(x_blocks, "gx")
    z_pieces = spread_rows(z_total, "gx")
    core_out = assemble(place, spread_rows(x_total, "gy"), z_pieces)
    return (q_first, q_second, core_out)


def solution(mesh):
    placed = (P("gx", "gz", "gy"), P("gy", None), P("gz", None), P(), P("gz", None))
    return jax.shard_map(
        on_device,
        mesh=mesh,
        in_specs=placed,
        out_specs=(P("gx", None), P("gy", None), P(("gx", "gy"), "gz", None)),
        check_vma=False,
    )
```

```python
import functools

import jax
import jax.numpy as jnp
from jax import lax
from jax.experimental import pallas as pl
from jax.experimental.pallas import tpu as pltpu
from jax.sharding import PartitionSpec as P

HIGHEST = lax.Precision.HIGHEST
LANES = 128
PANEL = 32
GROUP = 16
VMEM_BYTES = 28 * 2**20
VMEM_BYTES_SKETCH = 52 * 2**20
SMALL = pl.CostEstimate(flops=2**20, bytes_accessed=2**16, transcendentals=0)
FIRST_ROWS = (144, 192)
STEPS = 4
SENT = [(kind, shift, 0, 256) for kind in (0, 1) for shift in (0, 1, 3)]
SENT += [(kind, 2, FIRST_ROWS[kind], 256 - FIRST_ROWS[kind]) for kind in (0, 1)]


def dot_f32(a, b, contract):
    return lax.dot_general(
        a, b, (contract, ((), ())), precision=HIGHEST, preferred_element_type=jnp.float32
    )


def factor_inverse(work, inverse):
    n = work.shape[0]
    halves = n // LANES
    rows_at = lax.broadcasted_iota(jnp.int32, (n, n), 0)
    columns_at = lax.broadcasted_iota(jnp.int32, (n, n), 1)
    inverse[...] = jnp.where(rows_at == columns_at, 1.0, 0.0)
    row = lax.broadcasted_iota(jnp.int32, (PANEL, LANES), 0)
    for top in range(0, n, PANEL):
        half = top // LANES
        left = half * LANES
        bottom = top + PANEL
        tiles = [work[top:bottom, t * LANES : (t + 1) * LANES] for t in range(half, halves)]
        tiles += [inverse[top:bottom, t * LANES : (t + 1) * LANES] for t in range(half + 1)]
        pivots = jnp.ones((PANEL, LANES), jnp.float32)
        for start in range(0, PANEL, GROUP):
            first = top - left + start
            columns = [
                jnp.broadcast_to(tiles[0][:, first + m : first + m + 1], (PANEL, LANES))
                for m in range(GROUP)
            ]
            for m in range(GROUP):
                at = start + m
                pivot = columns[m][at : at + 1, :]
                pivots = jnp.where(row == at, pivot, pivots)
                factor = jnp.where(row > at, columns[m] * (1.0 / pivot), 0.0)
                for later in range(m + 1, GROUP):
                    columns[later] = columns[later] - factor * columns[later][at : at + 1, :]
                tiles = [tile - factor * tile[at : at + 1, :] for tile in tiles]
        scale = lax.rsqrt(pivots)
        tiles = [tile * scale for tile in tiles]
        kept = halves - half
        for t in range(half + 1):
            inverse[top:bottom, t * LANES : (t + 1) * LANES] = tiles[kept + t]
        if bottom < n:
            upper = jnp.concatenate(tiles[:kept], 1)
            solved = jnp.concatenate(tiles[kept:], 1)
            lower = upper.T[bottom - left :, :]
            work[bottom:, left:] = work[bottom:, left:] - dot_f32(lower, upper, ((1,), (0,)))
            inverse[bottom:, : left + LANES] = inverse[bottom:, : left + LANES] - dot_f32(
                lower, solved, ((1,), (0,))
            )


def split(x):
    high = x.astype(jnp.bfloat16)
    return high, (x - high.astype(jnp.float32)).astype(jnp.bfloat16)


def left_parts(x):
    high, low = split(x)
    return jnp.concatenate([high, high, low], 1)


def right_parts(x):
    high, low = split(x)
    return jnp.concatenate([high, low, high], 0)


def dot_parts(a, b):
    return jnp.dot(a, b, preferred_element_type=jnp.float32)


def place_rows(core, shares_ref, others_ref, all_ref):
    half = shares_ref.shape[1]
    for at in range(4):
        top = at * 2 * half
        mine = pl.multiple_of(top + core * half, half)
        other = pl.multiple_of(top + (1 - core) * half, half)
        all_ref[pl.ds(mine, half), :] = shares_ref[at]
        all_ref[pl.ds(other, half), :] = others_ref[at]


def first_orthonormal_kernel(place, *refs):
    shares, others, c_ref, q_ref, folded_ref, inverse_ref, all_ref, work = refs
    place_rows(place[2], shares, others, all_ref)
    rows = all_ref[...]
    n = rows.shape[1]
    work[...] = dot_f32(rows, rows, ((0,), (0,)))
    factor_inverse(work, inverse_ref)
    q = dot_f32(rows[:n], inverse_ref[...], ((1,), (1,)))
    q_ref[...] = q
    folded_ref[...] = dot_f32(c_ref[...], q, ((0,), (1,)))


def first_orthonormal(place, shares, sketch_c):
    _, half, n = shares[0].shape
    square = jax.ShapeDtypeStruct((n, n), jnp.float32)
    return pl.pallas_call(
        first_orthonormal_kernel,
        in_specs=[pl.BlockSpec(memory_space=pltpu.SMEM)]
        + [pl.BlockSpec(memory_space=pltpu.VMEM)] * 3,
        out_shape=[square] * 3 + [jax.ShapeDtypeStruct((8 * half, n), jnp.float32)],
        scratch_shapes=[pltpu.VMEM((n, n), jnp.float32)],
        compiler_params=pltpu.CompilerParams(vmem_limit_bytes=VMEM_BYTES_SKETCH),
        cost_estimate=SMALL,
        name="first_orthonormal",
    )(place, *shares, sketch_c)


def second_orthonormal_kernel(place, *refs):
    shares, others, q_ref, q_all_ref, all_ref, work, inverse = refs
    place_rows(place[2], shares, others, all_ref)
    rows = all_ref[...]
    n = rows.shape[1]
    work[...] = dot_f32(rows, rows, ((0,), (0,)))
    factor_inverse(work, inverse)
    q = dot_f32(rows, inverse[...], ((1,), (1,)))
    q_ref[...] = q[:n]
    q_all_ref[...] = q


def second_orthonormal(place, shares):
    _, half, n = shares[0].shape
    return pl.pallas_call(
        second_orthonormal_kernel,
        in_specs=[pl.BlockSpec(memory_space=pltpu.SMEM)]
        + [pl.BlockSpec(memory_space=pltpu.VMEM)] * 2,
        out_shape=[
            jax.ShapeDtypeStruct((n, n), jnp.float32),
            jax.ShapeDtypeStruct((8 * half, n), jnp.float32),
        ],
        scratch_shapes=[
            pltpu.VMEM((8 * half, n), jnp.float32),
            pltpu.VMEM((n, n), jnp.float32),
            pltpu.VMEM((n, n), jnp.float32),
        ],
        compiler_params=pltpu.CompilerParams(vmem_limit_bytes=VMEM_BYTES),
        cost_estimate=SMALL,
        name="second_orthonormal",
    )(place, *shares)


def first_slices_kernel(place, volume, *refs):
    outs, sems = refs[:2], refs[2]
    copies = []
    for kind, out in enumerate(outs):
        target = lax.rem(place[1 - kind] + 2, 4) * 8 + 32 * kind
        cells = pl.ds(pl.multiple_of(target, 8), 8)
        copies.append(
            pltpu.make_async_copy(
                volume.at[pl.ds(0, FIRST_ROWS[kind]), cells, :], out, sems.at[kind]
            )
        )
    for copy in copies:
        copy.start()
    for copy in copies:
        copy.wait()


def first_slices(place, volume):
    return pl.pallas_call(
        first_slices_kernel,
        in_specs=[
            pl.BlockSpec(memory_space=pltpu.SMEM),
            pl.BlockSpec(memory_space=pl.ANY),
        ],
        out_specs=[pl.BlockSpec(memory_space=pltpu.VMEM)] * 2,
        out_shape=[
            jax.ShapeDtypeStruct((rows, 8, volume.shape[2]), jnp.float32) for rows in FIRST_ROWS
        ],
        scratch_shapes=[pltpu.SemaphoreType.DMA((2,))],
        compiler_params=pltpu.CompilerParams(vmem_limit_bytes=VMEM_BYTES_SKETCH),
        cost_estimate=SMALL,
        name="first_slices",
    )(place, volume)


def first_sketch_kernel(place, v_ref, a_ref, b_ref, kept_ref, given_ref, *refs):
    sent, (parts, rows_ref, sems) = refs[: len(SENT)], refs[len(SENT) :]
    rows, depth, cols = v_ref.shape
    step = pl.program_id(0)
    steps = STEPS

    @pl.when(step == 0)
    def _():
        parts[...] = right_parts(a_ref[...])

    half_steps = steps // 2
    at = pl.ds(pl.multiple_of(lax.rem(step, half_steps) * rows, rows), rows)

    def copies_out(g):
        copies = []
        for key, (kind, shift, first, count) in enumerate(SENT):
            start, stop = max(first, g * rows), min(first + count, (g + 1) * rows)
            if start < stop:
                target = lax.rem(place[1 - kind] + shift, 4) * 8 + 32 * kind
                cells = pl.ds(pl.multiple_of(target, 8), 8)
                copies.append(
                    pltpu.make_async_copy(
                        v_ref.at[pl.ds(start - g * rows, stop - start), cells, :],
                        sent[key].at[pl.ds(start - first, stop - start)],
                        sems.at[key],
                    )
                )
        return copies

    for g in range(STEPS):

        @pl.when(step == g)
        def _():
            for copy in copies_out(g):
                copy.start()

    flat = v_ref.reshape(rows * depth, cols)
    weights = b_ref[...]
    for top in range(0, rows, 8):
        spread = dot_parts(left_parts(flat[top * depth : (top + 8) * depth, :]), parts[...])
        rows_ref[top : top + 8, :] = jnp.sum(spread.reshape(8, depth, -1) * weights[None], axis=1)

    @pl.when(step // half_steps == place[2])
    def _():
        kept_ref[at, :] = rows_ref[...]

    @pl.when(step // half_steps != place[2])
    def _():
        given_ref[at, :] = rows_ref[...]

    for g in range(STEPS):

        @pl.when(step == g)
        def _():
            for copy in copies_out(g):
                copy.wait()


def first_sketch(place, volume, sketch_a, sketch_b):
    rows, depth, cols = volume.shape
    rank = sketch_a.shape[1]
    step = rows // STEPS
    outs = pl.pallas_call(
        first_sketch_kernel,
        grid=(STEPS,),
        in_specs=[
            pl.BlockSpec(memory_space=pltpu.SMEM),
            pl.BlockSpec((step, depth, cols), lambda g: (g, 0, 0)),
            pl.BlockSpec(sketch_a.shape, lambda g: (0, 0)),
            pl.BlockSpec(sketch_b.shape, lambda g: (0, 0)),
        ],
        out_specs=[pl.BlockSpec((rows // 2, rank), lambda g: (0, 0))] * 2
        + [pl.BlockSpec(memory_space=pl.ANY)] * len(SENT),
        out_shape=[jax.ShapeDtypeStruct((rows // 2, rank), jnp.float32)] * 2
        + [
            jax.ShapeDtypeStruct((count, 8, cols), jnp.float32) for _, _, _, count in SENT
        ],
        scratch_shapes=[
            pltpu.VMEM((3 * cols, rank), jnp.bfloat16),
            pltpu.VMEM((step, rank), jnp.float32),
            pltpu.SemaphoreType.DMA((len(SENT),)),
        ],
        compiler_params=pltpu.CompilerParams(vmem_limit_bytes=VMEM_BYTES_SKETCH),
        cost_estimate=SMALL,
        name="first_sketch",
    )(place, volume, sketch_a, sketch_b)
    return outs[:2], {key[:3]: out for key, out in zip(SENT, outs[2:])}


def second_sketch_kernel(place, left_ref, right_ref, folded_ref, d_ref, *refs):
    kept_ref, given_ref, parts, total = refs
    rows, depth, _ = left_ref.shape

    @pl.when(pl.program_id(0) == 0)
    def _():
        parts[...] = left_parts(folded_ref[...])
        total[...] = jnp.zeros_like(total)

    weights = d_ref[...].T
    flats = [ref.reshape(rows * depth, LANES) for ref in (left_ref, right_ref)]
    for k in range(depth):
        cells = jnp.concatenate([flat[pl.ds(k, rows, stride=depth), :] for flat in flats], 1)
        mixed = dot_parts(parts[...], right_parts(cells))
        total[...] += mixed * weights[:, k : k + 1]

    @pl.when(pl.program_id(0) == pl.num_programs(0) - 1)
    def _():
        rows_ref = total
        rows_ref[...] = total[...].T
        half = kept_ref.shape[0]
        core = place[2]
        kept_ref[...] = rows_ref[pl.ds(pl.multiple_of(core * half, half), half), :]
        given_ref[...] = rows_ref[pl.ds(pl.multiple_of((1 - core) * half, half), half), :]


def second_sketch(place, volume, folded, sketch_d):
    rows, depth, cols = volume.shape
    rank = folded.shape[0]
    step = 8
    return pl.pallas_call(
        second_sketch_kernel,
        grid=(depth // step,),
        in_specs=[
            pl.BlockSpec(memory_space=pltpu.SMEM),
            pl.BlockSpec((rows, step, LANES), lambda g: (0, g, 0)),
            pl.BlockSpec((rows, step, LANES), lambda g: (0, g, 1)),
            pl.BlockSpec(folded.shape, lambda g: (0, 0)),
            pl.BlockSpec((step, rank), lambda g: (g, 0)),
        ],
        out_specs=[pl.BlockSpec((cols // 2, rank), lambda g: (0, 0))] * 2,
        out_shape=[jax.ShapeDtypeStruct((cols // 2, rank), jnp.float32)] * 2,
        scratch_shapes=[
            pltpu.VMEM((rank, 3 * rows), jnp.bfloat16),
            pltpu.VMEM((rank, cols), jnp.float32),
        ],
        compiler_params=pltpu.CompilerParams(vmem_limit_bytes=VMEM_BYTES_SKETCH),
        cost_estimate=SMALL,
        name="second_sketch",
    )(place, volume, volume, folded, sketch_d)


def factor_parts_kernel(place, inverse_ref, all_ref, x_ref, z_ref, by_x, by_z):
    rows = all_ref.shape[0] // 4
    for first in range(4):
        for second in range(4):
            block = lax.rem(place[0] + first, 4) * 64 + lax.rem(place[1] + second, 4) * 16
            moved = inverse_ref[pl.ds(pl.multiple_of(block, 16), 16), :]
            by_z[pl.ds(first * 64 + second * 16, 16), :] = moved
            by_x[pl.ds(second * 64 + first * 16, 16), :] = moved
    everything = all_ref[...]
    x_ref[...] = left_parts(dot_f32(by_z[...], everything[:rows], ((1,), (1,))))
    turned = dot_f32(by_x[...], everything, ((1,), (1,)))
    for s in range(4):
        z_ref[:, s * 3 * rows : (s + 1) * 3 * rows] = left_parts(turned[:, s * rows : (s + 1) * rows])


def factor_parts(place, inverse, all_rows):
    rank = all_rows.shape[1]
    rows = all_rows.shape[0] // 4
    return pl.pallas_call(
        factor_parts_kernel,
        in_specs=[pl.BlockSpec(memory_space=pltpu.SMEM)]
        + [pl.BlockSpec(memory_space=pltpu.VMEM)] * 2,
        out_shape=[
            jax.ShapeDtypeStruct((rank, 3 * rows), jnp.bfloat16),
            jax.ShapeDtypeStruct((rank, 12 * rows), jnp.bfloat16),
        ],
        scratch_shapes=[pltpu.VMEM((rank, rank), jnp.float32)] * 2,
        compiler_params=pltpu.CompilerParams(vmem_limit_bytes=VMEM_BYTES),
        cost_estimate=SMALL,
        name="factor_parts",
    )(place, inverse, all_rows)


def truncated_cell(q1_ref, source, flats, k):
    rows = flats[0].shape[0] // 8
    part = jnp.concatenate([flat[pl.ds(k, rows, stride=8), :] for flat in flats], 1)
    return dot_parts(q1_ref[:, source * 3 * rows : (source + 1) * 3 * rows], right_parts(part))


def lane_halves(held, at):
    rows = held.shape[1]
    return [held.at[2 * at + lane].reshape(rows * 8, LANES) for lane in range(2)]


def lane_copies(piece, held, at, rows, sems):
    return [
        pltpu.make_async_copy(
            piece.at[:, :, pl.ds(lane * LANES, LANES)], held.at[2 * at + lane, rows], sems.at[lane]
        )
        for lane in range(2)
    ]


def truncate_kernel(own, one, three, q1_ref, total, held, sems):
    everything = pl.ds(0, held.shape[1])
    copies = [
        lane_copies(piece, held, at, everything, sems.at[at])
        for at, piece in enumerate((own, one, three))
    ]
    for group in copies:
        for copy in group:
            copy.start()
    for at, source in enumerate((0, 1, 3)):
        for copy in copies[at]:
            copy.wait()
        flats = lane_halves(held, at)
        for k in range(8):
            product = truncated_cell(q1_ref, source, flats, k)
            total[k] = product if at == 0 else total[k] + product


def truncate(pieces, q1):
    rows, _, cols = pieces[0].shape
    return pl.pallas_call(
        truncate_kernel,
        in_specs=[pl.BlockSpec(memory_space=pl.ANY)] * 3
        + [pl.BlockSpec(memory_space=pltpu.VMEM)],
        out_shape=jax.ShapeDtypeStruct((8, q1.shape[0], cols), jnp.float32),
        scratch_shapes=[
            pltpu.VMEM((6, rows, 8, LANES), jnp.float32),
            pltpu.SemaphoreType.DMA((3, 2)),
        ],
        compiler_params=pltpu.CompilerParams(vmem_limit_bytes=VMEM_BYTES),
        cost_estimate=SMALL,
        name="truncate",
    )(*pieces, q1)


def finish_z_kernel(*refs):
    pieces, (t_ref, q1_ref, q2_ref) = refs[:2], refs[2:5]
    out_refs, (held, sems) = refs[5:9], refs[9:]
    copies = []
    first = 0
    for at, piece in enumerate(pieces):
        rows_at = pl.ds(first, piece.shape[0])
        copies += lane_copies(piece, held, 0, rows_at, sems.at[at])
        first += piece.shape[0]
    for copy in copies:
        copy.start()
    weights = right_parts(q2_ref[...])
    for copy in copies:
        copy.wait()
    flats = lane_halves(held, 0)
    share = out_refs[0].shape[1]
    for k in range(8):
        total = t_ref[k] + truncated_cell(q1_ref, 2, flats, k)
        product = dot_parts(left_parts(total), weights)
        for b in range(4):
            out_refs[b][k] = product[b * share : (b + 1) * share]


def finish_z(pieces, truncated, q1, q2):
    rows = sum(piece.shape[0] for piece in pieces)
    rank_first, rank_second = q1.shape[0], q2.shape[1]
    block = jax.ShapeDtypeStruct((8, rank_first // 4, rank_second), jnp.float32)
    return pl.pallas_call(
        finish_z_kernel,
        in_specs=[pl.BlockSpec(memory_space=pl.ANY)] * 2
        + [pl.BlockSpec(memory_space=pltpu.VMEM)] * 3,
        out_shape=[block] * 4,
        scratch_shapes=[
            pltpu.VMEM((2, rows, 8, LANES), jnp.float32),
            pltpu.SemaphoreType.DMA((2, 2)),
        ],
        compiler_params=pltpu.CompilerParams(vmem_limit_bytes=VMEM_BYTES),
        cost_estimate=SMALL,
        name="finish_z",
    )(*pieces, truncated, q1, q2)


def finish_x_kernel(*refs):
    (own, one, two, two_b, three, q1_ref, q2_ref), out_refs = refs[:7], refs[7:11]
    held, spread, weights, sems = refs[11:]
    rows = held.shape[2] * 2
    half = rows // 2
    copies = [[], []]
    over = two.shape[0] - half
    parts = [
        (part, source, piece.at[pl.ds(part * half, half)], 0)
        for part in range(2)
        for source, piece in ((0, own), (1, one), (3, three))
    ]
    parts += [(0, 2, two.at[pl.ds(0, half)], 0), (1, 2, two.at[pl.ds(half, over)], 0)]
    parts += [(1, 2, two_b, over)]
    for at, (part, source, piece, first) in enumerate(parts):
        to = held.at[source, part, pl.ds(first, piece.shape[0])]
        copies[part].append(pltpu.make_async_copy(piece, to, sems.at[at]))
    for copy in copies[0] + copies[1]:
        copy.start()
    cols = held.shape[4]
    for s in range(4):
        weights[s * 3 * cols : (s + 1) * 3 * cols, :] = right_parts(
            q2_ref[s * cols : (s + 1) * cols, :]
        )
    chunk = 256
    for part in range(2):
        for copy in copies[part]:
            copy.wait()
        for top in range(0, half * 8, chunk):
            lhs = jnp.concatenate(
                [
                    left_parts(held.at[s, part].reshape(half * 8, cols)[top : top + chunk, :])
                    for s in range(4)
                ],
                1,
            )
            mapped = dot_parts(lhs, weights[...])
            for lane in range(2):
                spread[lane, pl.ds(part * half * 8 + top, chunk), :] = mapped[
                    :, lane * LANES : (lane + 1) * LANES
                ]
    share = out_refs[0].shape[1]
    for k in range(8):
        mapped = jnp.concatenate(
            [spread.at[lane][pl.ds(k, rows, stride=8), :] for lane in range(2)], 1
        )
        product = dot_parts(q1_ref[...], right_parts(mapped))
        for b in range(4):
            out_refs[b][k] = product[b * share : (b + 1) * share]


def finish_x(pieces, q1, q2):
    rows, _, cols = pieces[0].shape
    rank_first, rank_second = q1.shape[0], q2.shape[1]
    block = jax.ShapeDtypeStruct((8, rank_first // 4, rank_second), jnp.float32)
    return pl.pallas_call(
        finish_x_kernel,
        in_specs=[pl.BlockSpec(memory_space=pl.ANY)] * 5
        + [pl.BlockSpec(memory_space=pltpu.VMEM)] * 2,
        out_shape=[block] * 4,
        scratch_shapes=[
            pltpu.VMEM((4, 2, rows // 2, 8, cols), jnp.float32),
            pltpu.VMEM((2, rows * 8, LANES), jnp.float32),
            pltpu.VMEM((12 * cols, rank_second), jnp.bfloat16),
            pltpu.SemaphoreType.DMA((9,)),
        ],
        compiler_params=pltpu.CompilerParams(vmem_limit_bytes=VMEM_BYTES),
        cost_estimate=SMALL,
        name="finish_x",
    )(*pieces, q1, q2)


def assemble_kernel(place, *refs):
    pieces, out_ref = refs[:8], refs[8]
    for b in range(4):
        x_cells = pl.ds(pl.multiple_of(lax.rem(place[1] + 4 - b, 4) * 8, 8), 8)
        z_cells = pl.ds(pl.multiple_of(32 + lax.rem(place[0] + 4 - b, 4) * 8, 8), 8)
        out_ref[:, x_cells, :] = jnp.swapaxes(pieces[b][...], 0, 1)
        out_ref[:, z_cells, :] = jnp.swapaxes(pieces[4 + b][...], 0, 1)


def assemble(place, x_pieces, z_pieces):
    _, rows, cols = x_pieces[0].shape
    return pl.pallas_call(
        assemble_kernel,
        in_specs=[pl.BlockSpec(memory_space=pltpu.SMEM)]
        + [pl.BlockSpec(memory_space=pltpu.VMEM)] * 8,
        out_shape=jax.ShapeDtypeStruct((rows, 64, cols), jnp.float32),
        compiler_params=pltpu.CompilerParams(vmem_limit_bytes=VMEM_BYTES),
        cost_estimate=SMALL,
        name="assemble",
    )(place, *x_pieces, *z_pieces)


def swap_cores(array):
    return lax.ppermute(array, "gz", [(i, i ^ 1) for i in range(lax.axis_size("gz"))])


def shifted(array, axis, step):
    size = lax.axis_size(axis)
    if axis == "gz":
        chips = size // 2
        pairs = [(i, ((i // 2 + step) % chips) * 2 + i % 2) for i in range(size)]
    else:
        pairs = [(i, (i + step) % size) for i in range(size)]
    return lax.ppermute(array, axis, pairs)


def sum_along(array, axis, beside=()):
    one, three, two = (shifted(array, axis, step) for step in (1, 3, 2))
    one, three, two, *beside = lax.optimization_barrier((one, three, two, *beside))
    return (array + two) + (one + three), beside


def behind(array, token):
    return lax.optimization_barrier((array, token))[0]


def gathered(mine, axis):
    received = [shifted(mine, axis, step) for step in (1, 2, 3)]
    shares = jnp.stack([mine, *received])
    return (shares, swap_cores(shares)), received


def scatter_sum(blocks, axis):
    one, three, two = (shifted(blocks[step], axis, step) for step in (1, 3, 2))
    return (blocks[0] + two) + (one + three)


def spread_rows(total, axis):
    share = total.shape[1] // 4
    blocks = [total[:, b * share : (b + 1) * share] for b in range(4)]
    return [blocks[0]] + [shifted(blocks[b], axis, b) for b in (1, 2, 3)]


def on_device(volume, sketch_a, sketch_b, sketch_c, sketch_d):
    place = jnp.stack(
        [lax.axis_index("gx"), lax.axis_index("gy"), lax.rem(lax.axis_index("gz"), 2)]
    ).astype(jnp.int32)
    axes = ("gy", "gx")
    moved = {}

    def send(token, kind, shift, first=0):
        piece = sent[kind, shift, first]
        moved[kind, shift, first] = shifted(behind(piece, token), axes[kind], shift)

    def arrived(array, *keys):
        held = lax.optimization_barrier((array, *(moved[key] for key in keys)))
        moved.update(zip(keys, held[1:]))
        return held[0]

    for kind, piece in enumerate(first_slices(place, volume)):
        moved[kind, 2, 0] = shifted(piece, axes[kind], 2)
    (kept, given), sent = first_sketch(place, volume, sketch_a, sketch_b)
    summed, _ = sum_along(kept + swap_cores(given), "gz")
    summed, _ = sum_along(arrived(summed, (0, 2, 0)), "gy")
    send(summed, 0, 1)
    send(summed, 0, 3)
    shares, received = gathered(arrived(summed, (1, 2, 0)), "gx")
    send(received, 1, 1)
    send(received, 1, 3)
    q_first, folded, inverse, all_first = first_orthonormal(place, shares, sketch_c)

    kept, given = second_sketch(place, volume, folded, sketch_d)
    summed = arrived(kept + swap_cores(given), (0, 1, 0), (0, 3, 0))
    q1 = factor_parts(place, behind(inverse, summed), all_first)
    summed, (q1_x, q1_z) = sum_along(summed, "gz", q1)
    summed = arrived(summed, (1, 1, 0), (1, 3, 0))
    ready = [sent[1, 0, 0], moved[1, 1, 0], moved[1, 3, 0]]
    truncated = truncate(ready, behind(q1_z, summed))
    summed, (truncated,) = sum_along(summed, "gx", [truncated])
    send(summed, 1, 2, FIRST_ROWS[1])
    shares, _ = gathered(summed, "gy")
    send(shares[1], 0, 2, FIRST_ROWS[0])
    q_second, q2 = second_orthonormal(place, shares)

    ready = [moved[1, 2, 0], moved[1, 2, FIRST_ROWS[1]]]
    z_blocks = finish_z(ready, truncated, q1_z, q_second)
    q2, z_first = lax.optimization_barrier((q2, z_blocks[0]))
    z_blocks = [z_first, *z_blocks[1:]]
    ready = [sent[0, 0, 0]]
    ready += [moved[0, 1, 0], moved[0, 2, 0], moved[0, 2, FIRST_ROWS[0]], moved[0, 3, 0]]
    x_blocks = finish_x(ready, q1_x, q2)
    z_total = scatter_sum(z_blocks, "gy")
    x_total = scatter_sum(x_blocks, "gx")
    z_pieces = spread_rows(z_total, "gx")
    core_out = assemble(place, spread_rows(x_total, "gy"), z_pieces)
    return (q_first, q_second, core_out)


def solution(mesh):
    placed = (P("gx", "gz", "gy"), P("gy", None), P("gz", None), P(), P("gz", None))
    return jax.shard_map(
        on_device,
        mesh=mesh,
        in_specs=placed,
        out_specs=(P("gx", None), P("gy", None), P(("gx", "gy"), "gz", None)),
        check_vma=False,
    )
```

```python
import functools

import jax
import jax.numpy as jnp
from jax import lax
from jax.experimental import pallas as pl
from jax.experimental.pallas import tpu as pltpu
from jax.sharding import PartitionSpec as P

HIGHEST = lax.Precision.HIGHEST
LANES = 128
PANEL = 32
GROUP = 16
VMEM_BYTES = 28 * 2**20
VMEM_BYTES_SKETCH = 44 * 2**20
SMALL = pl.CostEstimate(flops=2**20, bytes_accessed=2**16, transcendentals=0)
FIRST_ROWS = (144, 192)
STEPS = 4
SENT = [(kind, shift, 0, 256) for kind in (0, 1) for shift in (0, 1, 3)]
SENT += [(kind, 2, FIRST_ROWS[kind], 256 - FIRST_ROWS[kind]) for kind in (0, 1)]


def dot_f32(a, b, contract):
    return lax.dot_general(
        a, b, (contract, ((), ())), precision=HIGHEST, preferred_element_type=jnp.float32
    )


def factor_inverse(work, inverse):
    n = work.shape[0]
    halves = n // LANES
    rows_at = lax.broadcasted_iota(jnp.int32, (n, n), 0)
    columns_at = lax.broadcasted_iota(jnp.int32, (n, n), 1)
    inverse[...] = jnp.where(rows_at == columns_at, 1.0, 0.0)
    row = lax.broadcasted_iota(jnp.int32, (PANEL, LANES), 0)
    for top in range(0, n, PANEL):
        half = top // LANES
        left = half * LANES
        bottom = top + PANEL
        tiles = [work[top:bottom, t * LANES : (t + 1) * LANES] for t in range(half, halves)]
        tiles += [inverse[top:bottom, t * LANES : (t + 1) * LANES] for t in range(half + 1)]
        pivots = jnp.ones((PANEL, LANES), jnp.float32)
        for start in range(0, PANEL, GROUP):
            first = top - left + start
            columns = [
                jnp.broadcast_to(tiles[0][:, first + m : first + m + 1], (PANEL, LANES))
                for m in range(GROUP)
            ]
            for m in range(GROUP):
                at = start + m
                pivot = columns[m][at : at + 1, :]
                pivots = jnp.where(row == at, pivot, pivots)
                factor = jnp.where(row > at, columns[m] * (1.0 / pivot), 0.0)
                for later in range(m + 1, GROUP):
                    columns[later] = columns[later] - factor * columns[later][at : at + 1, :]
                tiles = [tile - factor * tile[at : at + 1, :] for tile in tiles]
        scale = lax.rsqrt(pivots)
        tiles = [tile * scale for tile in tiles]
        kept = halves - half
        for t in range(half + 1):
            inverse[top:bottom, t * LANES : (t + 1) * LANES] = tiles[kept + t]
        if bottom < n:
            upper = jnp.concatenate(tiles[:kept], 1)
            solved = jnp.concatenate(tiles[kept:], 1)
            lower = upper.T[bottom - left :, :]
            work[bottom:, left:] = work[bottom:, left:] - dot_f32(lower, upper, ((1,), (0,)))
            inverse[bottom:, : left + LANES] = inverse[bottom:, : left + LANES] - dot_f32(
                lower, solved, ((1,), (0,))
            )


def split(x):
    high = x.astype(jnp.bfloat16)
    return high, (x - high.astype(jnp.float32)).astype(jnp.bfloat16)


def left_parts(x):
    high, low = split(x)
    return jnp.concatenate([high, high, low], 1)


def right_parts(x):
    high, low = split(x)
    return jnp.concatenate([high, low, high], 0)


def dot_parts(a, b):
    return jnp.dot(a, b, preferred_element_type=jnp.float32)


def place_rows(core, shares_ref, others_ref, all_ref):
    half = shares_ref.shape[1]
    for at in range(4):
        top = at * 2 * half
        mine = pl.multiple_of(top + core * half, half)
        other = pl.multiple_of(top + (1 - core) * half, half)
        all_ref[pl.ds(mine, half), :] = shares_ref[at]
        all_ref[pl.ds(other, half), :] = others_ref[at]


def first_orthonormal_kernel(place, *refs):
    shares, others, c_ref, q_ref, folded_ref, inverse_ref, all_ref, work = refs
    place_rows(place[2], shares, others, all_ref)
    rows = all_ref[...]
    n = rows.shape[1]
    work[...] = dot_f32(rows, rows, ((0,), (0,)))
    factor_inverse(work, inverse_ref)
    q = dot_f32(rows[:n], inverse_ref[...], ((1,), (1,)))
    q_ref[...] = q
    folded_ref[...] = dot_f32(c_ref[...], q, ((0,), (1,)))


def first_orthonormal(place, shares, sketch_c):
    _, half, n = shares[0].shape
    square = jax.ShapeDtypeStruct((n, n), jnp.float32)
    return pl.pallas_call(
        first_orthonormal_kernel,
        in_specs=[pl.BlockSpec(memory_space=pltpu.SMEM)]
        + [pl.BlockSpec(memory_space=pltpu.VMEM)] * 3,
        out_shape=[square] * 3 + [jax.ShapeDtypeStruct((8 * half, n), jnp.float32)],
        scratch_shapes=[pltpu.VMEM((n, n), jnp.float32)],
        compiler_params=pltpu.CompilerParams(vmem_limit_bytes=VMEM_BYTES_SKETCH),
        cost_estimate=SMALL,
        name="first_orthonormal",
    )(place, *shares, sketch_c)


def second_orthonormal_kernel(place, *refs):
    shares, others, q_ref, q_all_ref, all_ref, work, inverse = refs
    place_rows(place[2], shares, others, all_ref)
    rows = all_ref[...]
    n = rows.shape[1]
    work[...] = dot_f32(rows, rows, ((0,), (0,)))
    factor_inverse(work, inverse)
    q = dot_f32(rows, inverse[...], ((1,), (1,)))
    q_ref[...] = q[:n]
    q_all_ref[...] = q


def second_orthonormal(place, shares):
    _, half, n = shares[0].shape
    return pl.pallas_call(
        second_orthonormal_kernel,
        in_specs=[pl.BlockSpec(memory_space=pltpu.SMEM)]
        + [pl.BlockSpec(memory_space=pltpu.VMEM)] * 2,
        out_shape=[
            jax.ShapeDtypeStruct((n, n), jnp.float32),
            jax.ShapeDtypeStruct((8 * half, n), jnp.float32),
        ],
        scratch_shapes=[
            pltpu.VMEM((8 * half, n), jnp.float32),
            pltpu.VMEM((n, n), jnp.float32),
            pltpu.VMEM((n, n), jnp.float32),
        ],
        compiler_params=pltpu.CompilerParams(vmem_limit_bytes=VMEM_BYTES),
        cost_estimate=SMALL,
        name="second_orthonormal",
    )(place, *shares)


def first_slices_kernel(place, volume, *refs):
    outs, sems = refs[:2], refs[2]
    copies = []
    for kind, out in enumerate(outs):
        target = lax.rem(place[1 - kind] + 2, 4) * 8 + 32 * kind
        cells = pl.ds(pl.multiple_of(target, 8), 8)
        copies.append(
            pltpu.make_async_copy(
                volume.at[pl.ds(0, FIRST_ROWS[kind]), cells, :], out, sems.at[kind]
            )
        )
    for copy in copies:
        copy.start()
    for copy in copies:
        copy.wait()


def first_slices(place, volume):
    return pl.pallas_call(
        first_slices_kernel,
        in_specs=[
            pl.BlockSpec(memory_space=pltpu.SMEM),
            pl.BlockSpec(memory_space=pl.ANY),
        ],
        out_specs=[pl.BlockSpec(memory_space=pltpu.VMEM)] * 2,
        out_shape=[
            jax.ShapeDtypeStruct((rows, 8, volume.shape[2]), jnp.float32) for rows in FIRST_ROWS
        ],
        scratch_shapes=[pltpu.SemaphoreType.DMA((2,))],
        compiler_params=pltpu.CompilerParams(vmem_limit_bytes=VMEM_BYTES_SKETCH),
        cost_estimate=SMALL,
        name="first_slices",
    )(place, volume)


def first_sketch_kernel(place, v_ref, a_ref, b_ref, kept_ref, given_ref, *refs):
    sent, (parts, rows_ref, sems) = refs[: len(SENT)], refs[len(SENT) :]
    rows, depth, cols = v_ref.shape
    step = pl.program_id(0)
    steps = STEPS

    @pl.when(step == 0)
    def _():
        parts[...] = right_parts(a_ref[...])

    half_steps = steps // 2
    at = pl.ds(pl.multiple_of(lax.rem(step, half_steps) * rows, rows), rows)

    def copies_out(g):
        copies = []
        for key, (kind, shift, first, count) in enumerate(SENT):
            start, stop = max(first, g * rows), min(first + count, (g + 1) * rows)
            if start < stop:
                target = lax.rem(place[1 - kind] + shift, 4) * 8 + 32 * kind
                cells = pl.ds(pl.multiple_of(target, 8), 8)
                copies.append(
                    pltpu.make_async_copy(
                        v_ref.at[pl.ds(start - g * rows, stop - start), cells, :],
                        sent[key].at[pl.ds(start - first, stop - start)],
                        sems.at[key],
                    )
                )
        return copies

    for g in range(STEPS):

        @pl.when(step == g)
        def _():
            for copy in copies_out(g):
                copy.start()

    flat = v_ref.reshape(rows * depth, cols)
    weights = b_ref[...]
    for top in range(0, rows, 8):
        spread = dot_parts(left_parts(flat[top * depth : (top + 8) * depth, :]), parts[...])
        rows_ref[top : top + 8, :] = jnp.sum(spread.reshape(8, depth, -1) * weights[None], axis=1)

    @pl.when(step // half_steps == place[2])
    def _():
        kept_ref[at, :] = rows_ref[...]

    @pl.when(step // half_steps != place[2])
    def _():
        given_ref[at, :] = rows_ref[...]

    for g in range(STEPS):

        @pl.when(step == g)
        def _():
            for copy in copies_out(g):
                copy.wait()


def first_sketch(place, volume, sketch_a, sketch_b):
    rows, depth, cols = volume.shape
    rank = sketch_a.shape[1]
    step = rows // STEPS
    outs = pl.pallas_call(
        first_sketch_kernel,
        grid=(STEPS,),
        in_specs=[
            pl.BlockSpec(memory_space=pltpu.SMEM),
            pl.BlockSpec((step, depth, cols), lambda g: (g, 0, 0)),
            pl.BlockSpec(sketch_a.shape, lambda g: (0, 0)),
            pl.BlockSpec(sketch_b.shape, lambda g: (0, 0)),
        ],
        out_specs=[pl.BlockSpec((rows // 2, rank), lambda g: (0, 0))] * 2
        + [pl.BlockSpec(memory_space=pl.ANY)] * len(SENT),
        out_shape=[jax.ShapeDtypeStruct((rows // 2, rank), jnp.float32)] * 2
        + [
            jax.ShapeDtypeStruct((count, 8, cols), jnp.float32) for _, _, _, count in SENT
        ],
        scratch_shapes=[
            pltpu.VMEM((3 * cols, rank), jnp.bfloat16),
            pltpu.VMEM((step, rank), jnp.float32),
            pltpu.SemaphoreType.DMA((len(SENT),)),
        ],
        compiler_params=pltpu.CompilerParams(vmem_limit_bytes=VMEM_BYTES_SKETCH),
        cost_estimate=SMALL,
        name="first_sketch",
    )(place, volume, sketch_a, sketch_b)
    return outs[:2], {key[:3]: out for key, out in zip(SENT, outs[2:])}


def second_sketch_kernel(place, left_ref, right_ref, folded_ref, d_ref, *refs):
    kept_ref, given_ref, parts, total = refs
    rows, depth, _ = left_ref.shape

    @pl.when(pl.program_id(0) == 0)
    def _():
        parts[...] = left_parts(folded_ref[...])
        total[...] = jnp.zeros_like(total)

    weights = d_ref[...].T
    flats = [ref.reshape(rows * depth, LANES) for ref in (left_ref, right_ref)]
    for k in range(depth):
        cells = jnp.concatenate([flat[pl.ds(k, rows, stride=depth), :] for flat in flats], 1)
        mixed = dot_parts(parts[...], right_parts(cells))
        total[...] += mixed * weights[:, k : k + 1]

    @pl.when(pl.program_id(0) == pl.num_programs(0) - 1)
    def _():
        rows_ref = total
        rows_ref[...] = total[...].T
        half = kept_ref.shape[0]
        core = place[2]
        kept_ref[...] = rows_ref[pl.ds(pl.multiple_of(core * half, half), half), :]
        given_ref[...] = rows_ref[pl.ds(pl.multiple_of((1 - core) * half, half), half), :]


def second_sketch(place, volume, folded, sketch_d):
    rows, depth, cols = volume.shape
    rank = folded.shape[0]
    step = 8
    return pl.pallas_call(
        second_sketch_kernel,
        grid=(depth // step,),
        in_specs=[
            pl.BlockSpec(memory_space=pltpu.SMEM),
            pl.BlockSpec((rows, step, LANES), lambda g: (0, g, 0)),
            pl.BlockSpec((rows, step, LANES), lambda g: (0, g, 1)),
            pl.BlockSpec(folded.shape, lambda g: (0, 0)),
            pl.BlockSpec((step, rank), lambda g: (g, 0)),
        ],
        out_specs=[pl.BlockSpec((cols // 2, rank), lambda g: (0, 0))] * 2,
        out_shape=[jax.ShapeDtypeStruct((cols // 2, rank), jnp.float32)] * 2,
        scratch_shapes=[
            pltpu.VMEM((rank, 3 * rows), jnp.bfloat16),
            pltpu.VMEM((rank, cols), jnp.float32),
        ],
        compiler_params=pltpu.CompilerParams(vmem_limit_bytes=VMEM_BYTES_SKETCH),
        cost_estimate=SMALL,
        name="second_sketch",
    )(place, volume, volume, folded, sketch_d)


def factor_parts_kernel(place, inverse_ref, all_ref, x_ref, z_ref, by_x, by_z):
    rows = all_ref.shape[0] // 4
    for first in range(4):
        for second in range(4):
            block = lax.rem(place[0] + first, 4) * 64 + lax.rem(place[1] + second, 4) * 16
            moved = inverse_ref[pl.ds(pl.multiple_of(block, 16), 16), :]
            by_z[pl.ds(first * 64 + second * 16, 16), :] = moved
            by_x[pl.ds(second * 64 + first * 16, 16), :] = moved
    everything = all_ref[...]
    x_ref[...] = left_parts(dot_f32(by_z[...], everything[:rows], ((1,), (1,))))
    turned = dot_f32(by_x[...], everything, ((1,), (1,)))
    for s in range(4):
        z_ref[:, s * 3 * rows : (s + 1) * 3 * rows] = left_parts(turned[:, s * rows : (s + 1) * rows])


def factor_parts(place, inverse, all_rows):
    rank = all_rows.shape[1]
    rows = all_rows.shape[0] // 4
    return pl.pallas_call(
        factor_parts_kernel,
        in_specs=[pl.BlockSpec(memory_space=pltpu.SMEM)]
        + [pl.BlockSpec(memory_space=pltpu.VMEM)] * 2,
        out_shape=[
            jax.ShapeDtypeStruct((rank, 3 * rows), jnp.bfloat16),
            jax.ShapeDtypeStruct((rank, 12 * rows), jnp.bfloat16),
        ],
        scratch_shapes=[pltpu.VMEM((rank, rank), jnp.float32)] * 2,
        compiler_params=pltpu.CompilerParams(vmem_limit_bytes=VMEM_BYTES),
        cost_estimate=SMALL,
        name="factor_parts",
    )(place, inverse, all_rows)


def truncated_cell(q1_ref, source, flats, k):
    rows = flats[0].shape[0] // 8
    part = jnp.concatenate([flat[pl.ds(k, rows, stride=8), :] for flat in flats], 1)
    return dot_parts(q1_ref[:, source * 3 * rows : (source + 1) * 3 * rows], right_parts(part))


def lane_halves(held, at):
    rows = held.shape[1]
    return [held.at[2 * at + lane].reshape(rows * 8, LANES) for lane in range(2)]


def lane_copies(piece, held, at, rows, sems):
    return [
        pltpu.make_async_copy(
            piece.at[:, :, pl.ds(lane * LANES, LANES)], held.at[2 * at + lane, rows], sems.at[lane]
        )
        for lane in range(2)
    ]


def truncate_kernel(own, one, three, q1_ref, total, held, sems):
    everything = pl.ds(0, held.shape[1])
    copies = [
        lane_copies(piece, held, at, everything, sems.at[at])
        for at, piece in enumerate((own, one, three))
    ]
    for group in copies:
        for copy in group:
            copy.start()
    for at, source in enumerate((0, 1, 3)):
        for copy in copies[at]:
            copy.wait()
        flats = lane_halves(held, at)
        for k in range(8):
            product = truncated_cell(q1_ref, source, flats, k)
            total[k] = product if at == 0 else total[k] + product


def truncate(pieces, q1):
    rows, _, cols = pieces[0].shape
    return pl.pallas_call(
        truncate_kernel,
        in_specs=[pl.BlockSpec(memory_space=pl.ANY)] * 3
        + [pl.BlockSpec(memory_space=pltpu.VMEM)],
        out_shape=jax.ShapeDtypeStruct((8, q1.shape[0], cols), jnp.float32),
        scratch_shapes=[
            pltpu.VMEM((6, rows, 8, LANES), jnp.float32),
            pltpu.SemaphoreType.DMA((3, 2)),
        ],
        compiler_params=pltpu.CompilerParams(vmem_limit_bytes=VMEM_BYTES),
        cost_estimate=SMALL,
        name="truncate",
    )(*pieces, q1)


def finish_z_kernel(*refs):
    pieces, (t_ref, q1_ref, q2_ref) = refs[:2], refs[2:5]
    out_refs, (held, sems) = refs[5:9], refs[9:]
    copies = []
    first = 0
    for at, piece in enumerate(pieces):
        rows_at = pl.ds(first, piece.shape[0])
        copies += lane_copies(piece, held, 0, rows_at, sems.at[at])
        first += piece.shape[0]
    for copy in copies:
        copy.start()
    weights = right_parts(q2_ref[: piece.shape[2], :])
    for copy in copies:
        copy.wait()
    flats = lane_halves(held, 0)
    share = out_refs[0].shape[1]
    for k in range(8):
        total = t_ref[k] + truncated_cell(q1_ref, 2, flats, k)
        product = dot_parts(left_parts(total), weights)
        for b in range(4):
            out_refs[b][k] = product[b * share : (b + 1) * share]


def finish_z(pieces, truncated, q1, q2):
    rows = sum(piece.shape[0] for piece in pieces)
    rank_first, rank_second = q1.shape[0], q2.shape[1]
    block = jax.ShapeDtypeStruct((8, rank_first // 4, rank_second), jnp.float32)
    return pl.pallas_call(
        finish_z_kernel,
        in_specs=[pl.BlockSpec(memory_space=pl.ANY)] * 2
        + [pl.BlockSpec(memory_space=pltpu.VMEM)] * 3,
        out_shape=[block] * 4,
        scratch_shapes=[
            pltpu.VMEM((2, rows, 8, LANES), jnp.float32),
            pltpu.SemaphoreType.DMA((2, 2)),
        ],
        compiler_params=pltpu.CompilerParams(vmem_limit_bytes=VMEM_BYTES),
        cost_estimate=SMALL,
        name="finish_z",
    )(*pieces, truncated, q1, q2)


def finish_x_kernel(*refs):
    (own, one, two, two_b, three, q1_ref, q2_ref), out_refs = refs[:7], refs[7:11]
    held, spread, weights, sems = refs[11:]
    rows = held.shape[2] * 2
    half = rows // 2
    copies = [[], []]
    over = two.shape[0] - half
    parts = [
        (part, source, piece.at[pl.ds(part * half, half)], 0)
        for part in range(2)
        for source, piece in ((0, own), (1, one), (3, three))
    ]
    parts += [(0, 2, two.at[pl.ds(0, half)], 0), (1, 2, two.at[pl.ds(half, over)], 0)]
    parts += [(1, 2, two_b, over)]
    for at, (part, source, piece, first) in enumerate(parts):
        to = held.at[source, part, pl.ds(first, piece.shape[0])]
        copies[part].append(pltpu.make_async_copy(piece, to, sems.at[at]))
    for copy in copies[0] + copies[1]:
        copy.start()
    cols = held.shape[4]
    for s in range(4):
        weights[s * 3 * cols : (s + 1) * 3 * cols, :] = right_parts(
            q2_ref[s * cols : (s + 1) * cols, :]
        )
    chunk = 256
    for part in range(2):
        for copy in copies[part]:
            copy.wait()
        for top in range(0, half * 8, chunk):
            lhs = jnp.concatenate(
                [
                    left_parts(held.at[s, part].reshape(half * 8, cols)[top : top + chunk, :])
                    for s in range(4)
                ],
                1,
            )
            mapped = dot_parts(lhs, weights[...])
            for lane in range(2):
                spread[lane, pl.ds(part * half * 8 + top, chunk), :] = mapped[
                    :, lane * LANES : (lane + 1) * LANES
                ]
    share = out_refs[0].shape[1]
    for k in range(8):
        mapped = jnp.concatenate(
            [spread.at[lane][pl.ds(k, rows, stride=8), :] for lane in range(2)], 1
        )
        product = dot_parts(q1_ref[...], right_parts(mapped))
        for b in range(4):
            out_refs[b][k] = product[b * share : (b + 1) * share]


def finish_x(pieces, q1, q2):
    rows, _, cols = pieces[0].shape
    rank_first, rank_second = q1.shape[0], q2.shape[1]
    block = jax.ShapeDtypeStruct((8, rank_first // 4, rank_second), jnp.float32)
    return pl.pallas_call(
        finish_x_kernel,
        in_specs=[pl.BlockSpec(memory_space=pl.ANY)] * 5
        + [pl.BlockSpec(memory_space=pltpu.VMEM)] * 2,
        out_shape=[block] * 4,
        scratch_shapes=[
            pltpu.VMEM((4, 2, rows // 2, 8, cols), jnp.float32),
            pltpu.VMEM((2, rows * 8, LANES), jnp.float32),
            pltpu.VMEM((12 * cols, rank_second), jnp.bfloat16),
            pltpu.SemaphoreType.DMA((9,)),
        ],
        compiler_params=pltpu.CompilerParams(vmem_limit_bytes=VMEM_BYTES),
        cost_estimate=SMALL,
        name="finish_x",
    )(*pieces, q1, q2)


def assemble_kernel(place, *refs):
    pieces, out_ref = refs[:8], refs[8]
    for b in range(4):
        x_cells = pl.ds(pl.multiple_of(lax.rem(place[1] + 4 - b, 4) * 8, 8), 8)
        z_cells = pl.ds(pl.multiple_of(32 + lax.rem(place[0] + 4 - b, 4) * 8, 8), 8)
        out_ref[:, x_cells, :] = jnp.swapaxes(pieces[b][...], 0, 1)
        out_ref[:, z_cells, :] = jnp.swapaxes(pieces[4 + b][...], 0, 1)


def assemble(place, x_pieces, z_pieces):
    _, rows, cols = x_pieces[0].shape
    return pl.pallas_call(
        assemble_kernel,
        in_specs=[pl.BlockSpec(memory_space=pltpu.SMEM)]
        + [pl.BlockSpec(memory_space=pltpu.VMEM)] * 8,
        out_shape=jax.ShapeDtypeStruct((rows, 64, cols), jnp.float32),
        compiler_params=pltpu.CompilerParams(vmem_limit_bytes=VMEM_BYTES),
        cost_estimate=SMALL,
        name="assemble",
    )(place, *x_pieces, *z_pieces)


def swap_cores(array):
    return lax.ppermute(array, "gz", [(i, i ^ 1) for i in range(lax.axis_size("gz"))])


def shifted(array, axis, step):
    size = lax.axis_size(axis)
    if axis == "gz":
        chips = size // 2
        pairs = [(i, ((i // 2 + step) % chips) * 2 + i % 2) for i in range(size)]
    else:
        pairs = [(i, (i + step) % size) for i in range(size)]
    return lax.ppermute(array, axis, pairs)


def sum_along(array, axis, beside=()):
    one, three, two = (shifted(array, axis, step) for step in (1, 3, 2))
    one, three, two, *beside = lax.optimization_barrier((one, three, two, *beside))
    return (array + two) + (one + three), beside


def behind(array, token):
    return lax.optimization_barrier((array, token))[0]


def gathered(mine, axis):
    received = [shifted(mine, axis, step) for step in (1, 2, 3)]
    shares = jnp.stack([mine, *received])
    return (shares, swap_cores(shares)), received


def scatter_sum(blocks, axis):
    one, three, two = (shifted(blocks[step], axis, step) for step in (1, 3, 2))
    return (blocks[0] + two) + (one + three)


def spread_rows(total, axis):
    share = total.shape[1] // 4
    blocks = [total[:, b * share : (b + 1) * share] for b in range(4)]
    return [blocks[0]] + [shifted(blocks[b], axis, b) for b in (1, 2, 3)]


def on_device(volume, sketch_a, sketch_b, sketch_c, sketch_d):
    place = jnp.stack(
        [lax.axis_index("gx"), lax.axis_index("gy"), lax.rem(lax.axis_index("gz"), 2)]
    ).astype(jnp.int32)
    axes = ("gy", "gx")
    moved = {}

    def send(token, kind, shift, first=0):
        piece = sent[kind, shift, first]
        moved[kind, shift, first] = shifted(behind(piece, token), axes[kind], shift)

    def arrived(array, *keys):
        held = lax.optimization_barrier((array, *(moved[key] for key in keys)))
        moved.update(zip(keys, held[1:]))
        return held[0]

    for kind, piece in enumerate(first_slices(place, volume)):
        moved[kind, 2, 0] = shifted(piece, axes[kind], 2)
    (kept, given), sent = first_sketch(place, volume, sketch_a, sketch_b)
    summed, _ = sum_along(kept + swap_cores(given), "gz")
    summed, _ = sum_along(arrived(summed, (0, 2, 0)), "gy")
    send(summed, 0, 1)
    send(summed, 0, 3)
    shares, received = gathered(arrived(summed, (1, 2, 0)), "gx")
    send(received, 1, 1)
    send(received, 1, 3)
    q_first, folded, inverse, all_first = first_orthonormal(place, shares, sketch_c)

    kept, given = second_sketch(place, volume, folded, sketch_d)
    summed = arrived(kept + swap_cores(given), (0, 1, 0), (0, 3, 0))
    q1 = factor_parts(place, behind(inverse, summed), all_first)
    summed, (q1_x, q1_z) = sum_along(summed, "gz", q1)
    summed = arrived(summed, (1, 1, 0), (1, 3, 0))
    ready = [sent[1, 0, 0], moved[1, 1, 0], moved[1, 3, 0]]
    truncated = truncate(ready, behind(q1_z, summed))
    summed, (truncated,) = sum_along(summed, "gx", [truncated])
    send(summed, 1, 2, FIRST_ROWS[1])
    shares, _ = gathered(summed, "gy")
    send(shares[1], 0, 2, FIRST_ROWS[0])
    q_second, q2 = second_orthonormal(place, shares)

    ready = [moved[1, 2, 0], moved[1, 2, FIRST_ROWS[1]]]
    z_blocks = finish_z(ready, truncated, q1_z, q2)
    q2, z_first = lax.optimization_barrier((q2, z_blocks[0]))
    z_blocks = [z_first, *z_blocks[1:]]
    ready = [sent[0, 0, 0]]
    ready += [moved[0, 1, 0], moved[0, 2, 0], moved[0, 2, FIRST_ROWS[0]], moved[0, 3, 0]]
    x_blocks = finish_x(ready, q1_x, q2)
    z_total = scatter_sum(z_blocks, "gy")
    x_total = scatter_sum(x_blocks, "gx")
    z_pieces = spread_rows(z_total, "gx")
    core_out = assemble(place, spread_rows(x_total, "gy"), z_pieces)
    return (q_first, q_second, core_out)


def solution(mesh):
    placed = (P("gx", "gz", "gy"), P("gy", None), P("gz", None), P(), P("gz", None))
    return jax.shard_map(
        on_device,
        mesh=mesh,
        in_specs=placed,
        out_specs=(P("gx", None), P("gy", None), P(("gx", "gy"), "gz", None)),
        check_vma=False,
    )
```
